32 devices in a mesh: tower: 2 (over x), grow: 4 (over y, core), gcol: 4 (over z).
Axes of the slice: x: 2, y: 2, z: 4, core: 2. Of those that a mesh axis runs over, the one named last changes fastest.
Arguments:
- hidden: bfloat16 [2, 4096, 768], P('tower', ('grow', 'gcol')), may hold values from -6 to 6
- preact: bfloat16 [2, 4096, 3072], P('tower', ('grow', 'gcol')), may hold values from -6 to 6
- w_down: bfloat16 [2, 768, 3072], P('tower', 'grow', 'gcol'), may hold values from -1 to 1
- projection: bfloat16 [2, 768, 768], P('tower', 'grow', 'gcol'), may hold values from -1 to 1
- log_scale: float32 [], replicated, may hold values from 4 to 6
Outputs:
- d_hidden: bfloat16 [2, 4096, 768], P('tower', ('grow', 'gcol'))
- d_preact: bfloat16 [2, 4096, 3072], P('tower', ('grow', 'gcol'))
- grad_down: float32 [2, 768, 3072], P('tower', 'grow', 'gcol')
- grad_proj: float32 [2, 768, 768], P('tower', 'grow', 'gcol')
The draws below stay inside these ranges and needn't reach their ends.
All inputs are finite; a program needn't handle non-finite values.
Results may differ from the reference program's by a relative error of at most 0.006.
The reference program's roundings to bfloat16 on the way count: a program that leaves them out, or rounds other values in their place, can miss the bound.
Values may be sent and summed in bfloat16 or wider, within the bound.
No kernel may reach another device: no remote copies, remote signals or barrier semaphores. Data moves between devices by JAX's collectives and lax.ppermute only.
A program may use at most 128 MiB of HBM per device.

```python
import math
import jax
import jax.numpy as jnp
from jax import lax

WIDTH = 768
INNER = 3072
EMBED = 768
BATCH = 4096


def draw_hidden(key, part):
    own_key = jax.random.fold_in(key, 1)
    key_image = jax.random.fold_in(own_key, 0)
    values = jnp.clip(jax.random.normal(key_image, (2, BATCH, WIDTH), jnp.float32), -6.0, 6.0)
    return values.astype(jnp.bfloat16)


def draw_preact(key, part):
    own_key = jax.random.fold_in(key, 2)
    key_image = jax.random.fold_in(own_key, 0)
    values = jnp.clip(jax.random.normal(key_image, (2, BATCH, INNER), jnp.float32), -6.0, 6.0)
    return values.astype(jnp.bfloat16)


def draw_w_down(key, part):
    own_key = jax.random.fold_in(key, 3)
    factor = float(INNER) ** (-0.5)
    values = jnp.clip(jax.random.normal(own_key, (2, WIDTH, INNER), jnp.float32), -4.0, 4.0) * factor
    return values.astype(jnp.bfloat16)


def draw_projection(key, part):
    own_key = jax.random.fold_in(key, 4)
    factor = float(WIDTH) ** (-0.5)
    values = jnp.clip(jax.random.normal(own_key, (2, WIDTH, EMBED), jnp.float32), -4.0, 4.0) * factor
    return values.astype(jnp.bfloat16)


def draw_log_scale(key, part):
    own_key = jax.random.fold_in(key, 5)
    value = jax.random.uniform(own_key, (), jnp.float32, 4.0, 4.6)
    return value.astype(jnp.float32)


def setup_inputs(seed: int = 0) -> dict:
    arg_keys = jax.random.split(jax.random.key(seed), 6)
    hidden = draw_hidden(jax.random.fold_in(arg_keys[5], 71), 0)
    preact = draw_preact(jax.random.fold_in(arg_keys[5], 71), 0)
    w_down = draw_w_down(jax.random.fold_in(arg_keys[5], 71), 0)
    projection = draw_projection(jax.random.fold_in(arg_keys[5], 71), 0)
    log_scale = draw_log_scale(jax.random.fold_in(arg_keys[5], 71), 0)
    return {"hidden": hidden, "preact": preact, "w_down": w_down, "projection": projection, "log_scale": log_scale}


def quick_gelu(values):
    return values * jax.nn.sigmoid(1.702 * values)

def gelu_slope(values):
    sigmoid = jax.nn.sigmoid(1.702 * values)
    return sigmoid + 1.702 * values * sigmoid * (1.0 - sigmoid)

def tower_forward(hidden_k, preact_k, down_k, proj_k):
    active = quick_gelu(preact_k.astype(jnp.float32)).astype(jnp.bfloat16)
    stream = hidden_k.astype(jnp.float32) + lax.dot_general(active, down_k, (((1,), (1,)), ((), ())), preferred_element_type=jnp.float32)
    stream_b = stream.astype(jnp.bfloat16)
    embed = jnp.dot(stream_b, proj_k, preferred_element_type=jnp.float32)
    inverse = lax.rsqrt(lax.optimization_barrier(jnp.sum(embed * embed, axis=1, keepdims=True)) + 1e-06)
    return (active, stream_b, embed * inverse, inverse)

def tower_backward(d_unit, unit, inverse, stream_b, active, preact_k, down_k, proj_k):
    inner = lax.optimization_barrier(jnp.sum(unit * d_unit, axis=1, keepdims=True))
    d_embed = (inverse * (d_unit - unit * inner)).astype(jnp.bfloat16)
    d_stream = lax.dot_general(d_embed, proj_k, (((1,), (1,)), ((), ())), preferred_element_type=jnp.float32).astype(jnp.bfloat16)
    d_active = jnp.dot(d_stream, down_k, preferred_element_type=jnp.float32)
    d_pre = (d_active * gelu_slope(preact_k.astype(jnp.float32))).astype(jnp.bfloat16)
    term_down = lax.dot_general(d_stream, active, (((0,), (0,)), ((), ())), preferred_element_type=jnp.float32)
    term_proj = lax.dot_general(stream_b, d_embed, (((0,), (0,)), ((), ())), preferred_element_type=jnp.float32)
    return (d_stream, d_pre, term_down, term_proj)

def reference(hidden, preact, w_down, projection, log_scale):
    logit_scale = jnp.exp(log_scale)
    forwards = [tower_forward(hidden[tower_id], preact[tower_id], w_down[tower_id], projection[tower_id]) for tower_id in range(2)]
    image_b = forwards[0][2].astype(jnp.bfloat16)
    text_b = forwards[1][2].astype(jnp.bfloat16)
    block_rows = math.gcd(BATCH, 1024)
    block_count = BATCH // block_rows
    indices = jnp.arange(block_count, dtype=jnp.int32)

    def block_scores(block_index):
        row_block = lax.dynamic_slice_in_dim(image_b, block_index * block_rows, block_rows, 0)
        scores = logit_scale * lax.dot_general(row_block, text_b, (((1,), (1,)), ((), ())), preferred_element_type=jnp.float32)
        return (row_block, scores)

    def first_pass(carry, block_index):
        column_max, column_sum = carry
        row_block, scores = block_scores(block_index)
        block_lse = jax.nn.logsumexp(scores, axis=1)
        joint_max = jnp.maximum(column_max, lax.optimization_barrier(jnp.max(scores, axis=0)))
        column_sum = column_sum * jnp.exp(column_max - joint_max) + lax.optimization_barrier(jnp.sum(jnp.exp(scores - joint_max[None, :]), axis=0))
        return ((joint_max, column_sum), block_lse)
    start_carry = (jnp.full((BATCH,), -1e+30, jnp.float32), jnp.zeros((BATCH,), jnp.float32))
    (column_max, column_sum), row_blocks = lax.scan(first_pass, start_carry, indices)
    row_lse = row_blocks.reshape(BATCH)
    column_lse = column_max + jnp.log(column_sum)
    column_ids = jnp.arange(BATCH, dtype=jnp.int32)

    def second_pass(text_grad, block_index):
        row_block, scores = block_scores(block_index)
        row_part = lax.dynamic_slice_in_dim(row_lse, block_index * block_rows, block_rows, 0)
        row_ids = block_index * block_rows + jnp.arange(block_rows, dtype=jnp.int32)
        diagonal = (row_ids[:, None] == column_ids[None, :]).astype(jnp.float32)
        grad = 0.5 * (jnp.exp(scores - row_part[:, None]) + jnp.exp(scores - column_lse[None, :])) - diagonal
        grad_b = grad.astype(jnp.bfloat16)
        image_block = logit_scale * jnp.dot(grad_b, text_b, preferred_element_type=jnp.float32)
        text_grad = text_grad + logit_scale * lax.dot_general(grad_b, row_block, (((0,), (0,)), ((), ())), preferred_element_type=jnp.float32)
        return (text_grad, image_block)
    text_grad, image_blocks = lax.scan(second_pass, jnp.zeros((BATCH, EMBED), jnp.float32), indices)
    image_grad = image_blocks.reshape(BATCH, EMBED)
    results = []
    for tower_id, d_unit in ((0, image_grad), (1, text_grad)):
        active, stream_b, unit, inverse = forwards[tower_id]
        results.append(tower_backward(d_unit, unit, inverse, stream_b, active, preact[tower_id], w_down[tower_id], projection[tower_id]))
    return (jnp.stack([results[0][0], results[1][0]]), jnp.stack([results[0][1], results[1][1]]), jnp.stack([results[0][2], results[1][2]]), jnp.stack([results[0][3], results[1][3]]))
```

```python
import jax
import jax.numpy as jnp
from jax import lax
from jax.sharding import PartitionSpec as P

F32 = jnp.float32
BF16 = jnp.bfloat16


def quick_gelu(values):
    return values * jax.nn.sigmoid(1.702 * values)


def gelu_slope(values):
    sigmoid = jax.nn.sigmoid(1.702 * values)
    return sigmoid + 1.702 * values * sigmoid * (1.0 - sigmoid)


def shift(value, axis, step):
    count = lax.axis_size(axis)
    return lax.ppermute(value, axis, [(i, (i + step) % count) for i in range(count)])


def swap(value, axis, bit):
    return lax.ppermute(value, axis, [(i, i ^ bit) for i in range(lax.axis_size(axis))])


def ring(value):
    blocks = [value]
    for _ in range(lax.axis_size("gcol") - 1):
        blocks.append(shift(blocks[-1], "gcol", 1))
    return blocks


def spread(blocks):
    table = {0: blocks}
    bit = lax.axis_size("grow") // 2
    while bit:
        for j in list(table):
            table[j ^ bit] = [swap(block, "grow", bit) for block in table[j]]
        bit //= 2
    return [table[j] for j in range(len(table))]


def gather_rows(value, chunks):
    parts = [spread(ring(part)) for part in jnp.split(value, chunks, 0)]
    grow_count, gcol_count = lax.axis_size("grow"), lax.axis_size("gcol")
    return [
        [[part[j][k] for part in parts] for k in range(gcol_count)] for j in range(grow_count)
    ]


def dot_tn(left, right):
    return lax.dot_general(left, right, (((0,), (0,)), ((), ())), preferred_element_type=F32)


def dot_nt(left, right):
    return lax.dot_general(left, right, (((1,), (1,)), ((), ())), preferred_element_type=F32)


def dot_nn(left, right):
    return jnp.dot(left, right, preferred_element_type=F32)


def body(hidden, preact, w_down, projection, log_scale):
    tower_count = lax.axis_size("tower")
    grow_count, gcol_count = lax.axis_size("grow"), lax.axis_size("gcol")
    tower, grow, gcol = (lax.axis_index(a) for a in ("tower", "grow", "gcol"))
    hidden, preact, w_down, projection = hidden[0], preact[0], w_down[0], projection[0]
    rows = hidden.shape[0]
    features, inner_block = w_down.shape
    columns = projection.shape[1]
    js, ks = range(grow_count), range(gcol_count)

    proj_pieces = gather_rows(projection, 1)
    down_pieces = gather_rows(w_down, 2)
    down = [jnp.concatenate([part for j in js for part in down_pieces[j][k]], 0) for k in ks]
    proj = jnp.concatenate(
        [jnp.concatenate([proj_pieces[j][k][0] for j in js], 0) for k in reversed(ks)], 1
    )
    proj = jnp.roll(proj, (gcol + 1) * columns, 1)

    place = [lax.rem(gcol - k + gcol_count, gcol_count) * inner_block for k in ks]
    pre = [lax.dynamic_slice_in_dim(preact, place[k], inner_block, 1).astype(F32) for k in ks]
    active = [quick_gelu(pre[k]).astype(BF16) for k in ks]
    hidden_rel = jnp.concatenate(
        [lax.dynamic_slice_in_dim(hidden, (grow ^ j) * features, features, 1) for j in js], 1
    )
    stream = hidden_rel.astype(F32) + sum(dot_nt(active[k], down[k]) for k in ks)
    stream_b = stream.astype(BF16)
    embed = dot_nn(stream_b, proj)
    inverse = lax.rsqrt(jnp.sum(embed * embed, axis=1, keepdims=True) + 1e-06)
    unit = embed * inverse
    unit_b = unit.astype(BF16)

    chunks = 2
    pieces = [
        spread(ring(swap(part, "tower", 1))) for part in jnp.split(unit_b, chunks, 0)
    ]
    order = [(j, k) for j in js for k in ks]
    others = jnp.concatenate([pieces[q][j][k] for j, k in order for q in range(chunks)], 0)
    logit_scale = jnp.exp(log_scale)
    scores = logit_scale * dot_nt(unit_b, others)
    row_max = jnp.max(scores, axis=1)
    row_lse = row_max + jnp.log(jnp.sum(jnp.exp(scores - row_max[:, None]), axis=1))

    active_all = spread([jnp.concatenate(active, 1)])
    stream_all = [
        swap(stream_b[:, j * features : (j + 1) * features], "grow", j) if j else stream_b[:, :features]
        for j in js
    ]

    device_count = tower_count * grow_count * gcol_count
    lse_all = lax.all_to_all(
        jnp.broadcast_to(row_lse[None], (device_count, rows)), ("tower", "grow", "gcol"), 0, 0
    )
    sources = jnp.stack(
        [
            ((1 - tower) * grow_count + (grow ^ j)) * gcol_count
            + lax.rem(gcol - k + gcol_count, gcol_count)
            for j, k in order
        ]
    )
    other_lse = jnp.take(lse_all, sources, axis=0).reshape(-1)

    row_index = lax.broadcasted_iota(jnp.int32, scores.shape, 0)
    column_index = lax.broadcasted_iota(jnp.int32, scores.shape, 1)
    grad = 0.5 * (
        jnp.exp(scores - row_lse[:, None]) + jnp.exp(scores - other_lse[None, :])
    ) - (row_index == column_index).astype(F32)
    d_unit = logit_scale * dot_nn(grad.astype(BF16), others)
    along = jnp.sum(unit * d_unit, axis=1, keepdims=True)
    d_embed = (inverse * (d_unit - unit * along)).astype(BF16)
    d_stream = dot_nt(d_embed, proj).astype(BF16)

    d_embed_all = [table[0] for table in spread([d_embed])]
    d_stream_all = [
        swap(d_stream[:, j * features : (j + 1) * features], "grow", j) if j else d_stream[:, :features]
        for j in js
    ]
    left = jnp.concatenate(d_stream_all, 0)
    active_rows = jnp.concatenate([table[0] for table in active_all], 0)
    term_proj = dot_tn(jnp.concatenate(stream_all, 0), jnp.concatenate(d_embed_all, 0))
    grad_down, grad_proj = None, None
    sent = []
    for k in ks:
        term = dot_tn(left, active_rows[:, k * inner_block : (k + 1) * inner_block])
        owner = lax.rem(gcol - k + gcol_count, gcol_count)
        term_p = lax.dynamic_slice_in_dim(term_proj, owner * columns, columns, 1)
        if k == 0:
            grad_down, grad_proj = term, term_p
        else:
            sent.append((shift(term.astype(BF16), "gcol", -k), shift(term_p.astype(BF16), "gcol", -k)))
    for term, term_p in sent:
        grad_down = grad_down + term.astype(F32)
        grad_proj = grad_proj + term_p.astype(F32)

    d_pre = jnp.zeros(preact.shape, BF16)
    for k in ks:
        part = (dot_nn(d_stream, down[k]) * gelu_slope(pre[k])).astype(BF16)
        d_pre = lax.dynamic_update_slice_in_dim(d_pre, part, place[k], 1)
    d_hidden = jnp.zeros(hidden.shape, BF16)
    for j in js:
        d_hidden = lax.dynamic_update_slice_in_dim(
            d_hidden, d_stream[:, j * features : (j + 1) * features], (grow ^ j) * features, 1
        )
    return (d_hidden[None], d_pre[None], grad_down[None], grad_proj[None])


def solution(mesh):
    placed = (
        P("tower", ("grow", "gcol"), None),
        P("tower", ("grow", "gcol"), None),
        P("tower", "grow", "gcol"),
        P("tower", "grow", "gcol"),
        P(),
    )
    return jax.shard_map(
        body, mesh=mesh, in_specs=placed, out_specs=placed[:4], check_vma=False
    )
```

```python
import jax
import jax.numpy as jnp
from jax import lax
from jax.experimental import pallas as pl
from jax.experimental.pallas import tpu as pltpu
from jax.sharding import PartitionSpec as P

F32 = jnp.float32
BF16 = jnp.bfloat16


def quick_gelu(values):
    return values * jax.nn.sigmoid(1.702 * values)


def gelu_slope(values):
    sigmoid = jax.nn.sigmoid(1.702 * values)
    return sigmoid + 1.702 * values * sigmoid * (1.0 - sigmoid)


def shift(value, axis, step):
    count = lax.axis_size(axis)
    return lax.ppermute(value, axis, [(i, (i + step) % count) for i in range(count)])


def swap(value, axis, bit):
    return lax.ppermute(value, axis, [(i, i ^ bit) for i in range(lax.axis_size(axis))])


def ring(value, *earlier):
    blocks = [value]
    for step in range(1, lax.axis_size("gcol")):
        part = after(blocks[-1], *earlier) if step == 2 and earlier else blocks[-1]
        blocks.append(shift(part, "gcol", 1))
    return blocks


def grow_bits(last):
    bits, bit = [], lax.axis_size("grow") // 2
    while bit >= last:
        bits.append(bit)
        bit //= 2
    return bits


class Lane:
    def __init__(self):
        self.last = None

    def __call__(self, value, bit, *earlier):
        if self.last is not None:
            earlier = (*earlier, self.last)
        if earlier:
            value = after(value, *earlier)
        self.last = swap(value, "grow", bit)
        return self.last


def spread(value, lane=None, *earlier):
    table = {0: value}
    for bit in grow_bits(2):
        for j in list(table):
            table[j ^ bit] = lane(table[j], bit, *earlier) if lane else swap(table[j], "grow", bit)
    return table


def after(value, *earlier):
    return lax.optimization_barrier((value, *earlier))[0]


def dot_tn(left, right):
    return lax.dot_general(left, right, (((0,), (0,)), ((), ())), preferred_element_type=F32)


def dot_nt(left, right):
    return lax.dot_general(left, right, (((1,), (1,)), ((), ())), preferred_element_type=F32)


def dot_nn(left, right):
    return jnp.dot(left, right, preferred_element_type=F32)


def call(kernel, outs, *operands, name, in_specs=None, scalars=0):
    vmem, smem = pl.BlockSpec(memory_space=pltpu.VMEM), pl.BlockSpec(memory_space=pltpu.SMEM)
    specs = [smem] * scalars + [vmem] * (len(operands) - scalars)
    for place, spec in (in_specs or {}).items():
        specs[place] = spec
    return pl.pallas_call(
        kernel,
        out_shape=[jax.ShapeDtypeStruct(shape, dtype) for shape, dtype in outs],
        in_specs=specs,
        out_specs=[vmem] * len(outs),
        compiler_params=pltpu.CompilerParams(vmem_limit_bytes=56 * 1024 * 1024),
        cost_estimate=pl.CostEstimate(flops=1, bytes_accessed=1, transcendentals=0),
        name=name,
    )(*operands)


def activate(places, preact, block):
    rows, inner = preact.shape
    count = inner // block

    def kernel(places_ref, preact_ref, *outs):
        for k in range(count):
            start = pl.multiple_of(places_ref[k] * block, 128)
            outs[k][...] = quick_gelu(preact_ref[:, pl.ds(start, block)].astype(F32)).astype(BF16)

    outs = [((rows, block), BF16)] * count
    return call(kernel, outs, places, preact, name="activate", scalars=1)


def score_rows(log_scale, mine, mate, others, device_count):
    rows = mine.shape[0]
    width = others.shape[0]

    def kernel(scale_ref, mine_ref, mate_ref, others_ref, scores_mine, scores_mate, lse):
        halves = (scores_mine, scores_mate)
        logit_scale = scale_ref[0, 0]
        for half, ref in enumerate((mine_ref, mate_ref)):
            scores = halves[half]
            largest = None
            for place in range(0, width, 256):
                part = logit_scale * dot_nt(ref[...], others_ref[place : place + 256])
                scores[:, place : place + 256] = part
                here = jnp.max(part, axis=1, keepdims=True)
                largest = here if largest is None else jnp.maximum(largest, here)
            total = jnp.zeros_like(largest)
            for place in range(0, width, 256):
                part = scores[:, place : place + 256]
                total += jnp.sum(jnp.exp(part - largest), axis=1, keepdims=True)
            value = jnp.broadcast_to(largest + jnp.log(total), (rows, 128))
            row = value.T[:1]
            for device in range(device_count):
                lse[device, :, half * rows : (half + 1) * rows] = row

    outs = [((rows, width), F32)] * 2 + [((device_count, 1, 2 * rows), F32)]
    scale = jnp.exp(log_scale).reshape(1, 1)
    return call(kernel, outs, scale, mine, mate, others, name="scores", scalars=1)


def combine_lse(where, lse_all, count):
    rows = lse_all.shape[2] // 2

    def kernel(where_ref, lse_ref, column, row):
        def part(place, side):
            return lse_ref[where_ref[place]][:, side * rows : (side + 1) * rows]

        def log_add(left, right):
            top = jnp.maximum(left, right)
            return top + jnp.log(jnp.exp(left - top) + jnp.exp(right - top))

        for side in range(2):
            own = log_add(part(0, side), part(1, 1 - side))
            column[side * rows : (side + 1) * rows] = jnp.broadcast_to(own, (128, rows)).T[:, :1]
        for step in range(count):
            other = log_add(part(2 + 2 * step, 0), part(3 + 2 * step, 1))
            row[:, step * rows : (step + 1) * rows] = other

    outs = [((2 * rows, 1), F32), ((1, count * rows), F32)]
    return call(kernel, outs, where, lse_all, name="combine", scalars=1)


def all_terms(places, proj_own, rights, streams, embeds, columns):
    pieces, depth, width = len(embeds), proj_own.shape[0], rights[0][0].shape[1]
    rows, count = embeds[0].shape[0], len(rights) + 1

    def kernel(places_ref, proj_ref, *refs):
        embeds, refs = refs[:pieces], refs[pieces:]
        groups = [refs[pieces * i : pieces * (i + 1)] for i in range(len(rights))]
        streams, outs = refs[pieces * len(rights) :][: pieces // 2], refs[pieces * len(rights) + pieces // 2 :]
        left = outs[-1]
        for i, ref in enumerate(embeds):
            turned = dot_nt(proj_ref[...], ref[...]).astype(BF16)
            left[:, i * rows : (i + 1) * rows] = turned
        for i, group in enumerate(groups):
            total = None
            for j, ref in enumerate(group):
                part = dot_nn(left[:, j * rows : (j + 1) * rows], ref[...])
                total = part if total is None else total + part
            outs[i][:, :width] = total.astype(BF16)
        total = None
        for j, ref in enumerate(embeds):
            start = j % 2 * rows
            part = dot_nn(streams[j // 2][start : start + rows].T, ref[...])
            total = part if total is None else total + part
        for place in range(count):
            part = total[:, place * columns : (place + 1) * columns]
            for i in range(len(rights)):

                @pl.when(places_ref[i + 1] == place)
                def _():
                    outs[i][:, width:] = part.astype(BF16)

            @pl.when(places_ref[0] == place)
            def _():
                outs[-2][...] = part

    outs = [((depth, width + columns), BF16)] * len(rights)
    outs += [((depth, columns), F32), ((depth, rows * pieces), BF16)]
    flat = [piece for right in rights for piece in right]
    result = call(kernel, outs, places, proj_own, *embeds, *flat, *streams, name="terms", scalars=1)
    return result[:-2], result[-2], result[-1]


def weight_terms(left, right):
    depth, rows = left.shape[0], right[0].shape[0]

    def kernel(left_ref, *refs):
        out = refs[-1]
        total = None
        for j, ref in enumerate(refs[:-1]):
            part = dot_nn(left_ref[:, j * rows : (j + 1) * rows], ref[...])
            total = part if total is None else total + part
        out[...] = total

    return call(kernel, [((depth, right[0].shape[1]), F32)], left, *right, name="down_own")[0]


def own_gradients(places, found, preact, d_embed, d_stream, proj_mine, proj_rest, down_mine, down_rest):
    rows, inner = preact.shape
    blocks, features = len(d_stream), d_stream[0].shape[1]
    count, block = len(down_mine), down_mine[0].shape[1]
    depth, half = proj_mine.shape[0], blocks // 2

    def kernel(places_ref, found_ref, preact_ref, embed_ref, proj_a, proj_b, *refs):
        stream, refs = refs[:blocks], refs[blocks:]
        down_a, down_b, (d_hidden, d_pre) = refs[:count], refs[count : 2 * count], refs[2 * count :]
        for i in range(blocks):
            place = found_ref[i]
            near = place < half
            start = pl.multiple_of(jnp.where(near, place, place - half) * features, 16)
            rows_a, rows_b = proj_a[pl.ds(start, features)], proj_b[pl.ds(start, features)]
            part = dot_nt(embed_ref[...], jnp.where(near, rows_a, rows_b)).astype(BF16)
            d_hidden[:, i * features : (i + 1) * features] = part
        left = jnp.concatenate([r[...] for r in stream], 1)
        for k in range(count):
            start = pl.multiple_of(places_ref[k] * block, 128)
            d_active = dot_nn(left[:, :depth], down_a[k][...]) + dot_nn(left[:, depth:], down_b[k][...])
            slope = gelu_slope(preact_ref[:, pl.ds(start, block)].astype(F32))
            d_pre[:, pl.ds(start, block)] = (d_active * slope).astype(BF16)

    return call(
        kernel, [((rows, blocks * features), BF16), (preact.shape, BF16)], places, found, preact, d_embed,
        proj_mine, proj_rest, *d_stream, *down_mine, *down_rest, name="own_gradients", scalars=2,
    )


def body(hidden, preact, w_down, projection, log_scale):
    tower_count = lax.axis_size("tower")
    grow_count, gcol_count = lax.axis_size("grow"), lax.axis_size("gcol")
    tower, grow, gcol = (lax.axis_index(a) for a in ("tower", "grow", "gcol"))
    hidden, preact, w_down, projection = hidden[0], preact[0], w_down[0], projection[0]
    features, inner_block = w_down.shape
    columns = projection.shape[1]
    js, ks = range(grow_count), range(gcol_count)
    evens = range(0, grow_count, 2)
    last = evens[-1]
    order = [(j, k) for j in evens for k in ks]
    sources = [lax.rem(gcol - k + gcol_count, gcol_count) for k in ks]
    far, core = (Lane(), Lane()), Lane()
    places = jnp.stack(sources)
    found = [((grow ^ j) >> 1) + ((grow ^ j) & 1) * (grow_count // 2) for j in js]
    places, found = lax.optimization_barrier((places, jnp.stack(found)))
    chunks = range(2)

    active = activate(places, preact, inner_block)
    down_ring = ring(w_down)
    proj_ring = [projection]
    for k in ks[1:]:
        pace = () if k == 1 else (down_ring[k - 1],)
        proj_ring.append(shift(after(proj_ring[-1], *pace), "gcol", 1))
    down_tables = [spread(part, far[0]) for part in down_ring]
    active_even = {0: spread(active[0], None)}
    proj_own = jnp.roll(jnp.concatenate(proj_ring[::-1], 1), (gcol + 1) * columns, 1)
    proj_even = spread(proj_own)
    proj_pair = jnp.concatenate([proj_even[j] for j in evens], 0)
    proj_mate = swap(proj_pair, "grow", 1)
    proj_all = jnp.concatenate([proj_pair, proj_mate], 0)
    down_pair = [jnp.concatenate([table[j] for j in evens], 0) for table in down_tables]
    active_mate = [core(part, 1) for part in active]
    hidden_parts = [
        lax.dynamic_slice_in_dim(hidden, (grow ^ j) * features, features, 1) for j in js
    ]
    hidden_mine = jnp.concatenate([hidden_parts[j] for j in evens], 1)
    hidden_mate = core(jnp.concatenate([hidden_parts[j + 1] for j in evens], 1), 1)

    stream = jnp.concatenate([hidden_mine, hidden_mate], 0).astype(F32)
    stream = stream + sum(
        dot_nt(jnp.concatenate([active[k], active_mate[k]], 0), down_pair[k]) for k in ks
    )
    stream = stream.astype(BF16)
    own_rows = hidden.shape[0]
    stream_rest = swap(stream[own_rows:], "grow", 1)
    stream_b = jnp.concatenate([stream[:own_rows], stream_rest], 1)
    embed = after(dot_nn(stream_b, proj_all), active_even[0][last])
    inverse = lax.rsqrt(jnp.sum(embed * embed, axis=1, keepdims=True) + 1e-06)
    unit = embed * inverse
    unit_b = unit.astype(BF16)

    (
        unit, unit_b, inverse, stream, proj_pair, proj_mate, proj_all, down_pair, active, active_mate, preact, active_even
    ) = lax.optimization_barrier(
        (unit, unit_b, inverse, stream, proj_pair, proj_mate, proj_all, down_pair, active, active_mate, preact, active_even)
    )
    far, core = (Lane(), Lane()), Lane()
    active_even[1] = spread(active[1])

    unit_mate = swap(unit_b, "grow", 1)
    rings = [
        ring(after(swap(part, "tower", 1), active_even[1][last]))
        for part in jnp.split(unit_b, 2, 0)
    ]
    pieces = {(k, q): spread(rings[q][k], far[q]) for k in ks for q in chunks}
    others = jnp.concatenate([pieces[k, q][j] for j, k in order for q in chunks], 0)
    device_count = tower_count * grow_count * gcol_count
    others, unit_mate, unit_b, active_even, stream, active, log_scale = lax.optimization_barrier(
        (others, unit_mate, unit_b, active_even, stream, active, log_scale)
    )
    scores_own, scores_mate, lse = score_rows(log_scale, unit_b, unit_mate, others, device_count)
    lse_all = lax.all_to_all(lse, ("tower", "grow", "gcol"), 0, 0)

    far = (Lane(), Lane())
    for k in ks[2:]:
        active_even[k] = spread(active[k])
    stream_blocks = [stream[:, i * features : (i + 1) * features] for i in range(len(evens))]
    stream_even = {0: stream_blocks[0]}
    for i, j in enumerate(evens[1:], 1):
        stream_even[j] = swap(stream_blocks[i], "grow", j)
    core = Lane()
    active_odd = {k: {j: core(active_even[k][j], 1, others) for j in evens[1:]} for k in ks}

    def device(tower_of, j, k):
        return (tower_of * grow_count + (grow ^ j)) * gcol_count + sources[k]

    where = [device(tower, 0, 0), device(tower, 1, 0)]
    for j, k in order:
        where += [device(1 - tower, j, k), device(1 - tower, j ^ 1, k)]
    row_lse, other_lse = combine_lse(jnp.stack(where), lse_all, len(order))
    logit_scale = jnp.exp(log_scale)

    def embed_gradient(part, lse, diagonal):
        grad = 0.5 * (jnp.exp(part - lse) + jnp.exp(part - other_lse))
        return logit_scale * dot_nn((grad - diagonal).astype(BF16), others)

    row_index = lax.broadcasted_iota(jnp.int32, scores_own.shape, 0)
    column_index = lax.broadcasted_iota(jnp.int32, scores_own.shape, 1)
    diagonal = (row_index == column_index).astype(F32)
    arrived = [stream_even[last]] + [active_even[k][last] for k in ks[2:]]
    for_mate = embed_gradient(after(scores_mate, *arrived), row_lse[own_rows:], 0.0)
    for_own = embed_gradient(after(scores_own, for_mate), row_lse[:own_rows], diagonal)
    d_unit = for_own + swap(for_mate, "grow", 1)
    along = jnp.sum(unit * d_unit, axis=1, keepdims=True)
    d_embed = (inverse * (d_unit - unit * along)).astype(BF16)
    for_barrier = (d_embed, active_even, active_odd, stream_even, down_pair, proj_all, for_mate)
    for_barrier = lax.optimization_barrier(for_barrier)
    d_embed, active_even, active_odd, stream_even, down_pair, proj_all, for_mate = for_barrier
    rel = [*evens, *(j + 1 for j in evens)]
    d_stream = [
        dot_nt(d_embed, proj_all[i * features : (i + 1) * features]).astype(BF16) for i in js
    ]
    rights = []
    for k in ks:
        parts = {0: active[k], 1: active_mate[k]}
        for j in evens[1:]:
            parts[j], parts[j + 1] = active_even[k][j], active_odd[k][j]
        rights.append([parts[j] for j in js])
    embed_rows = {}
    for j, part in spread(d_embed).items():
        embed_rows[j], embed_rows[j + 1] = part, swap(part, "grow", 1)
    away = [*ks[1:]]
    terms, grad_proj, left = all_terms(
        places, proj_pair[:features], [rights[k] for k in away], [stream_even[j] for j in evens],
        [embed_rows[j] for j in js], columns,
    )
    sent = [shift(term, "gcol", -k) for k, term in zip(away, terms)]
    rights[0][0] = after(rights[0][0], *terms)
    grad_down = weight_terms(left, rights[0])

    down_mate = [swap(after(part, *terms), "grow", 1) for part in down_pair]
    d_hidden, d_pre = own_gradients(
        places, found, preact, after(d_embed, *terms), d_stream, proj_pair, proj_mate, down_pair, down_mate
    )
    grad_down, grad_proj = after(grad_down, d_pre, d_hidden), after(grad_proj, d_pre, d_hidden)
    for part in sent:
        grad_down = grad_down + part[:, :inner_block].astype(F32)
        grad_proj = grad_proj + part[:, inner_block:].astype(F32)
    return (d_hidden[None], d_pre[None], grad_down[None], grad_proj[None])


def solution(mesh):
    placed = (
        P("tower", ("grow", "gcol"), None),
        P("tower", ("grow", "gcol"), None),
        P("tower", "grow", "gcol"),
        P("tower", "grow", "gcol"),
        P(),
    )
    return jax.shard_map(
        body, mesh=mesh, in_specs=placed, out_specs=placed[:4], check_vma=False
    )
```

```python
import math

import jax
import jax.numpy as jnp
from jax import lax
from jax.experimental import pallas as pl
from jax.experimental.pallas import tpu as pltpu
from jax.sharding import PartitionSpec as P

F32 = jnp.float32
BF16 = jnp.bfloat16


def quick_gelu(values):
    return values * jax.nn.sigmoid(1.702 * values)


def gelu_slope(values):
    sigmoid = jax.nn.sigmoid(1.702 * values)
    return sigmoid + 1.702 * values * sigmoid * (1.0 - sigmoid)


def shift(value, axis, step):
    count = lax.axis_size(axis)
    return lax.ppermute(value, axis, [(i, (i + step) % count) for i in range(count)])


def swap(value, axis, bit):
    return lax.ppermute(value, axis, [(i, i ^ bit) for i in range(lax.axis_size(axis))])


def ring(value, *earlier):
    blocks = [value]
    for step in range(1, lax.axis_size("gcol")):
        part = after(blocks[-1], *earlier) if step == 2 and earlier else blocks[-1]
        blocks.append(shift(part, "gcol", 1))
    return blocks


def shift_across(value):
    towers, count = lax.axis_size("tower"), lax.axis_size("gcol")
    pairs = [
        (t * count + c, (towers - 1 - t) * count + (c + 1) % count)
        for t in range(towers)
        for c in range(count)
    ]
    return lax.ppermute(value, ("tower", "gcol"), pairs)


def swap_across(value):
    towers = lax.axis_size("tower")
    return lax.ppermute(value, "tower", [(t, towers - 1 - t) for t in range(towers)])


def grow_bits(last):
    bits, bit = [], lax.axis_size("grow") // 2
    while bit >= last:
        bits.append(bit)
        bit //= 2
    return bits


class Lane:
    def __init__(self):
        self.last = None

    def __call__(self, value, bit, *earlier):
        if self.last is not None:
            earlier = (*earlier, self.last)
        if earlier:
            value = after(value, *earlier)
        self.last = swap(value, "grow", bit)
        return self.last


def spread(value, lane=None, *earlier):
    table = {0: value}
    for bit in grow_bits(2):
        for j in list(table):
            table[j ^ bit] = lane(table[j], bit, *earlier) if lane else swap(table[j], "grow", bit)
    return table


def after(value, *earlier):
    return lax.optimization_barrier((value, *earlier))[0]


def dot_tn(left, right):
    return lax.dot_general(left, right, (((0,), (0,)), ((), ())), preferred_element_type=F32)


def dot_nt(left, right):
    return lax.dot_general(left, right, (((1,), (1,)), ((), ())), preferred_element_type=F32)


def dot_nn(left, right):
    return jnp.dot(left, right, preferred_element_type=F32)


def call(kernel, outs, *operands, name, in_specs=None, scalars=0):
    vmem, smem = pl.BlockSpec(memory_space=pltpu.VMEM), pl.BlockSpec(memory_space=pltpu.SMEM)
    specs = [smem] * scalars + [vmem] * (len(operands) - scalars)
    for place, spec in (in_specs or {}).items():
        specs[place] = spec
    held = sum(math.prod(shape) * jnp.dtype(dtype).itemsize for shape, dtype in outs)
    held += sum(value.size * value.dtype.itemsize for value in operands)
    return pl.pallas_call(
        kernel,
        out_shape=[jax.ShapeDtypeStruct(shape, dtype) for shape, dtype in outs],
        in_specs=specs,
        out_specs=[vmem] * len(outs),
        compiler_params=pltpu.CompilerParams(vmem_limit_bytes=min(held + 12 * 2**20, 56 * 2**20)),
        cost_estimate=pl.CostEstimate(flops=1, bytes_accessed=1, transcendentals=0),
        name=name,
    )(*operands)


def activate(places, preact, block):
    rows, inner = preact.shape
    count = inner // block

    def kernel(places_ref, preact_ref, *outs):
        for k in range(count):
            start = pl.multiple_of(places_ref[k] * block, 128)
            outs[k][...] = quick_gelu(preact_ref[:, pl.ds(start, block)].astype(F32)).astype(BF16)

    outs = [((rows, block), BF16)] * count
    return call(kernel, outs, places, preact, name="activate", scalars=1)


def score_rows(log_scale, mine, mate, others, device_count):
    rows = mine.shape[0]
    width = others.shape[0]

    def kernel(scale_ref, mine_ref, mate_ref, others_ref, scores_mine, scores_mate, lse):
        halves = (scores_mine, scores_mate)
        logit_scale = scale_ref[0, 0]
        for half, ref in enumerate((mine_ref, mate_ref)):
            scores = halves[half]
            largest = None
            for place in range(0, width, 256):
                part = logit_scale * dot_nt(ref[...], others_ref[place : place + 256])
                scores[:, place : place + 256] = part
                here = jnp.max(part, axis=1, keepdims=True)
                largest = here if largest is None else jnp.maximum(largest, here)
            total = jnp.zeros_like(largest)
            for place in range(0, width, 256):
                part = scores[:, place : place + 256]
                total += jnp.sum(jnp.exp(part - largest), axis=1, keepdims=True)
            value = jnp.broadcast_to(largest + jnp.log(total), (rows, 128))
            row = value.T[:1]
            for device in range(device_count):
                lse[device, :, half * rows : (half + 1) * rows] = row

    outs = [((rows, width), F32)] * 2 + [((device_count, 1, 2 * rows), F32)]
    scale = jnp.exp(log_scale).reshape(1, 1)
    return call(kernel, outs, scale, mine, mate, others, name="scores", scalars=1)


def combine_lse(where, lse_all, count):
    rows = lse_all.shape[2] // 2

    def kernel(where_ref, lse_ref, column, row):
        def part(place, side):
            return lse_ref[where_ref[place]][:, side * rows : (side + 1) * rows]

        def log_add(left, right):
            top = jnp.maximum(left, right)
            return top + jnp.log(jnp.exp(left - top) + jnp.exp(right - top))

        for side in range(2):
            own = log_add(part(0, side), part(1, 1 - side))
            column[side * rows : (side + 1) * rows] = jnp.broadcast_to(own, (128, rows)).T[:, :1]
        for step in range(count):
            other = log_add(part(2 + 2 * step, 0), part(3 + 2 * step, 1))
            row[:, step * rows : (step + 1) * rows] = other

    outs = [((2 * rows, 1), F32), ((1, count * rows), F32)]
    return call(kernel, outs, where, lse_all, name="combine", scalars=1)


def all_terms(places, proj_own, rights, streams, embeds, columns):
    pieces, depth, width = len(embeds), proj_own.shape[0], rights[0][0].shape[1]
    rows, count = embeds[0].shape[0], len(rights) + 1

    def kernel(places_ref, proj_ref, *refs):
        embeds, refs = refs[:pieces], refs[pieces:]
        groups = [refs[pieces * i : pieces * (i + 1)] for i in range(len(rights))]
        streams, outs = refs[pieces * len(rights) :][: pieces // 2], refs[pieces * len(rights) + pieces // 2 :]
        left = outs[-1]
        for i, ref in enumerate(embeds):
            turned = dot_nt(proj_ref[...], ref[...]).astype(BF16)
            left[:, i * rows : (i + 1) * rows] = turned
        for i, group in enumerate(groups):
            total = None
            for j, ref in enumerate(group):
                part = dot_nn(left[:, j * rows : (j + 1) * rows], ref[...])
                total = part if total is None else total + part
            outs[i][:, :width] = total.astype(BF16)
        total = None
        for j, ref in enumerate(embeds):
            start = j % 2 * rows
            part = dot_nn(streams[j // 2][start : start + rows].T, ref[...])
            total = part if total is None else total + part
        for place in range(count):
            part = total[:, place * columns : (place + 1) * columns]
            for i in range(len(rights)):

                @pl.when(places_ref[i + 1] == place)
                def _():
                    outs[i][:, width:] = part.astype(BF16)

            @pl.when(places_ref[0] == place)
            def _():
                outs[-2][...] = part

    outs = [((depth, width + columns), BF16)] * len(rights)
    outs += [((depth, columns), F32), ((depth, rows * pieces), BF16)]
    flat = [piece for right in rights for piece in right]
    result = call(kernel, outs, places, proj_own, *embeds, *flat, *streams, name="terms", scalars=1)
    return result[:-2], result[-2], result[-1]


def weight_terms(left, right):
    depth, rows = left.shape[0], right[0].shape[0]

    def kernel(left_ref, *refs):
        out = refs[-1]
        total = None
        for j, ref in enumerate(refs[:-1]):
            part = dot_nn(left_ref[:, j * rows : (j + 1) * rows], ref[...])
            total = part if total is None else total + part
        out[...] = total

    return call(kernel, [((depth, right[0].shape[1]), F32)], left, *right, name="down_own")[0]


def own_gradients(places, found, preact, d_embed, proj_mine, proj_rest, down_mine, down_rest):
    rows, inner = preact.shape
    blocks = found.shape[0]
    count, block = len(down_mine), down_mine[0].shape[1]
    depth, half = proj_mine.shape[0], blocks // 2
    features = depth // half

    def kernel(places_ref, found_ref, preact_ref, embed_ref, proj_a, proj_b, *refs):
        down_a, down_b, (d_hidden, d_pre) = refs[:count], refs[count : 2 * count], refs[2 * count :]
        for i in range(blocks):
            place = found_ref[i]
            near = place < half
            start = pl.multiple_of(jnp.where(near, place, place - half) * features, 16)
            rows_a, rows_b = proj_a[pl.ds(start, features)], proj_b[pl.ds(start, features)]
            part = dot_nt(embed_ref[...], jnp.where(near, rows_a, rows_b)).astype(BF16)
            d_hidden[:, i * features : (i + 1) * features] = part
        left_a = dot_nt(embed_ref[...], proj_a[...]).astype(BF16)
        left_b = dot_nt(embed_ref[...], proj_b[...]).astype(BF16)
        for k in range(count):
            start = pl.multiple_of(places_ref[k] * block, 128)
            d_active = dot_nn(left_a, down_a[k][...]) + dot_nn(left_b, down_b[k][...])
            slope = gelu_slope(preact_ref[:, pl.ds(start, block)].astype(F32))
            d_pre[:, pl.ds(start, block)] = (d_active * slope).astype(BF16)

    return call(
        kernel, [((rows, blocks * features), BF16), (preact.shape, BF16)], places, found, preact, d_embed,
        proj_mine, proj_rest, *down_mine, *down_rest, name="own_gradients", scalars=2,
    )


def body(hidden, preact, w_down, projection, log_scale):
    tower_count = lax.axis_size("tower")
    grow_count, gcol_count = lax.axis_size("grow"), lax.axis_size("gcol")
    tower, grow, gcol = (lax.axis_index(a) for a in ("tower", "grow", "gcol"))
    hidden, preact, w_down, projection = hidden[0], preact[0], w_down[0], projection[0]
    features, inner_block = w_down.shape
    columns = projection.shape[1]
    js, ks = range(grow_count), range(gcol_count)
    evens = range(0, grow_count, 2)
    last = evens[-1]
    order = [(j, k) for j in evens for k in ks]
    sources = [lax.rem(gcol - k + gcol_count, gcol_count) for k in ks]
    far, core = (Lane(), Lane()), Lane()
    places = jnp.stack(sources)
    found = [((grow ^ j) >> 1) + ((grow ^ j) & 1) * (grow_count // 2) for j in js]
    places, found = lax.optimization_barrier((places, jnp.stack(found)))
    chunks = range(2)

    active = activate(places, preact, inner_block)
    down_ring = ring(w_down)
    proj_ring = [projection]
    for k in ks[1:]:
        pace = () if k == 1 else (down_ring[k - 1],)
        proj_ring.append(shift(after(proj_ring[-1], *pace), "gcol", 1))
    down_tables = [spread(part, far[0]) for part in down_ring]
    active_even = {1: spread(active[1])}
    proj_own = jnp.roll(jnp.concatenate(proj_ring[::-1], 1), (gcol + 1) * columns, 1)
    proj_even = spread(proj_own)
    proj_pair = jnp.concatenate([proj_even[j] for j in evens], 0)
    proj_mate = swap(proj_pair, "grow", 1)
    proj_all = jnp.concatenate([proj_pair, proj_mate], 0)
    down_pair = [jnp.concatenate([table[j] for j in evens], 0) for table in down_tables]
    active_mate = [core(part, 1) for part in active]
    hidden_parts = [
        lax.dynamic_slice_in_dim(hidden, (grow ^ j) * features, features, 1) for j in js
    ]
    hidden_mine = jnp.concatenate([hidden_parts[j] for j in evens], 1)
    hidden_mate = core(jnp.concatenate([hidden_parts[j + 1] for j in evens], 1), 1)

    stream = jnp.concatenate([hidden_mine, hidden_mate], 0).astype(F32)
    stream = stream + sum(
        dot_nt(jnp.concatenate([active[k], active_mate[k]], 0), down_pair[k]) for k in ks
    )
    stream = stream.astype(BF16)
    own_rows = hidden.shape[0]
    stream_rest = swap(stream[own_rows:], "grow", 1)
    stream_b = jnp.concatenate([stream[:own_rows], stream_rest], 1)
    embed = after(dot_nn(stream_b, proj_all), active_even[1][last])
    inverse = lax.rsqrt(jnp.sum(embed * embed, axis=1, keepdims=True) + 1e-06)
    unit = embed * inverse
    unit_b = unit.astype(BF16)

    (
        unit, unit_b, inverse, stream, proj_pair, proj_mate, proj_all, down_pair, active, active_mate, preact, active_even
    ) = lax.optimization_barrier(
        (unit, unit_b, inverse, stream, proj_pair, proj_mate, proj_all, down_pair, active, active_mate, preact, active_even)
    )
    far, core = (Lane(), Lane()), Lane()

    stream_blocks = [stream[:, i * features : (i + 1) * features] for i in range(len(evens))]
    stream_even = {0: stream_blocks[0]}
    for i, j in enumerate(evens[1:], 1):
        stream_even[j] = swap(stream_blocks[i], "grow", j)
    across = swap_across(unit_b)
    near = {j: swap_across(part) for j, part in spread(unit_b).items() if j}
    near[0] = across
    rings = []
    for part in jnp.split(unit_b, 2, 0):
        blocks = [None, shift_across(part)]
        for k in ks[2:]:
            pace = (across, stream_even[last]) if k == 3 else ()
            blocks.append(shift(after(blocks[-1], *pace), "gcol", 1))
        rings.append(blocks)
    unit_mate = swap(after(unit_b, rings[0][-1]), "grow", 1)
    pieces = [near] + [
        spread(jnp.concatenate([rings[q][k] for q in chunks], 0)) for k in ks[1:-1]
    ]
    lasts = [spread(after(rings[q][-1], pieces[1][last], near[last])) for q in chunks]
    pieces.append({j: jnp.concatenate([part[j] for part in lasts], 0) for j in evens})
    others = jnp.concatenate([pieces[k][j] for j, k in order], 0)
    device_count = tower_count * grow_count * gcol_count
    others, unit_mate, unit_b, active_even, stream_even, active, log_scale = lax.optimization_barrier(
        (others, unit_mate, unit_b, active_even, stream_even, active, log_scale)
    )
    scores_own, scores_mate, lse = score_rows(log_scale, unit_b, unit_mate, others, device_count)
    lse_all = lax.all_to_all(lse, ("tower", "grow", "gcol"), 0, 0)

    far = (Lane(), Lane())
    for k in ks[2:]:
        active_even[k] = spread(active[k])
    core = Lane()
    active_odd = {k: {j: core(active_even[k][j], 1, others) for j in evens[1:]} for k in ks[1:]}

    def device(tower_of, j, k):
        return (tower_of * grow_count + (grow ^ j)) * gcol_count + sources[k]

    where = [device(tower, 0, 0), device(tower, 1, 0)]
    for j, k in order:
        where += [device(1 - tower, j, k), device(1 - tower, j ^ 1, k)]
    row_lse, other_lse = combine_lse(jnp.stack(where), lse_all, len(order))
    logit_scale = jnp.exp(log_scale)

    def embed_gradient(part, lse, diagonal):
        grad = 0.5 * (jnp.exp(part - lse) + jnp.exp(part - other_lse))
        return logit_scale * dot_nn((grad - diagonal).astype(BF16), others)

    row_index = lax.broadcasted_iota(jnp.int32, scores_own.shape, 0)
    column_index = lax.broadcasted_iota(jnp.int32, scores_own.shape, 1)
    diagonal = (row_index == column_index).astype(F32)
    arrived = [active_even[k][last] for k in ks[2:]]
    scores_mate, scores_own, row_lse = lax.optimization_barrier((scores_mate, scores_own, row_lse))
    for_mate = embed_gradient(after(scores_mate, *arrived), row_lse[own_rows:], 0.0)
    for_own = embed_gradient(after(scores_own, for_mate), row_lse[:own_rows], diagonal)
    d_unit = for_own + swap(for_mate, "grow", 1)
    along = jnp.sum(unit * d_unit, axis=1, keepdims=True)
    d_embed = (inverse * (d_unit - unit * along)).astype(BF16)
    for_barrier = (d_embed, active_even, active_odd, stream_even, down_pair, proj_all, for_mate)
    for_barrier = lax.optimization_barrier(for_barrier)
    d_embed, active_even, active_odd, stream_even, down_pair, proj_all, for_mate = for_barrier

    def right(k, even, odd):
        parts = {0: active[k], 1: active_mate[k]}
        for j in evens[1:]:
            parts[j], parts[j + 1] = even[j], odd[j]
        return [parts[j] for j in js]

    rights = {k: right(k, active_even[k], active_odd[k]) for k in ks[1:]}
    embed_rows = {}
    for j, part in spread(d_embed).items():
        embed_rows[j], embed_rows[j + 1] = part, swap(part, "grow", 1)
    down_mate = [swap(part, "grow", 1) for part in down_pair]
    away = [*ks[1:]]
    terms, grad_proj, left = all_terms(
        places, after(proj_pair[:features], *down_mate), [rights[k] for k in away], [stream_even[j] for j in evens],
        [embed_rows[j] for j in js], columns,
    )
    sent = [shift(term, "gcol", -k) for k, term in zip(away, terms)]
    even = spread(after(active[0], *terms))
    odd = {j: swap(even[j], "grow", 1) for j in evens[1:]}
    grad_down = weight_terms(left, right(0, even, odd))

    d_hidden, d_pre = own_gradients(
        places, found, preact, after(d_embed, *terms), proj_pair, proj_mate, down_pair, down_mate
    )
    grad_down, grad_proj = after(grad_down, d_pre, d_hidden), after(grad_proj, d_pre, d_hidden)
    for part in sent:
        grad_down = grad_down + part[:, :inner_block].astype(F32)
        grad_proj = grad_proj + part[:, inner_block:].astype(F32)
    return (d_hidden[None], d_pre[None], grad_down[None], grad_proj[None])


def solution(mesh):
    placed = (
        P("tower", ("grow", "gcol"), None),
        P("tower", ("grow", "gcol"), None),
        P("tower", "grow", "gcol"),
        P("tower", "grow", "gcol"),
        P(),
    )
    return jax.shard_map(
        body, mesh=mesh, in_specs=placed, out_specs=placed[:4], check_vma=False
    )
```

```python
import math

import jax
import jax.numpy as jnp
from jax import lax
from jax.experimental import pallas as pl
from jax.experimental.pallas import tpu as pltpu
from jax.sharding import PartitionSpec as P

F32 = jnp.float32
BF16 = jnp.bfloat16


def quick_gelu(values):
    return values * jax.nn.sigmoid(1.702 * values)


def gelu_slope(values):
    sigmoid = jax.nn.sigmoid(1.702 * values)
    return sigmoid + 1.702 * values * sigmoid * (1.0 - sigmoid)


def shift(value, axis, step):
    count = lax.axis_size(axis)
    return lax.ppermute(value, axis, [(i, (i + step) % count) for i in range(count)])


def swap(value, axis, bit):
    return lax.ppermute(value, axis, [(i, i ^ bit) for i in range(lax.axis_size(axis))])


def ring(value, *earlier):
    blocks = [value]
    for step in range(1, lax.axis_size("gcol")):
        part = after(blocks[-1], *earlier) if step == 2 and earlier else blocks[-1]
        blocks.append(shift(part, "gcol", 1))
    return blocks


def shift_across(value):
    towers, count = lax.axis_size("tower"), lax.axis_size("gcol")
    pairs = [
        (t * count + c, (towers - 1 - t) * count + (c + 1) % count)
        for t in range(towers)
        for c in range(count)
    ]
    return lax.ppermute(value, ("tower", "gcol"), pairs)


def swap_across(value):
    towers = lax.axis_size("tower")
    return lax.ppermute(value, "tower", [(t, towers - 1 - t) for t in range(towers)])


def grow_bits(last):
    bits, bit = [], lax.axis_size("grow") // 2
    while bit >= last:
        bits.append(bit)
        bit //= 2
    return bits


class Lane:
    def __init__(self):
        self.last = None

    def __call__(self, value, bit, *earlier):
        if self.last is not None:
            earlier = (*earlier, self.last)
        if earlier:
            value = after(value, *earlier)
        self.last = swap(value, "grow", bit)
        return self.last


def spread(value, lane=None, *earlier):
    table = {0: value}
    for bit in grow_bits(2):
        for j in list(table):
            table[j ^ bit] = lane(table[j], bit, *earlier) if lane else swap(table[j], "grow", bit)
    return table


def after(value, *earlier):
    return lax.optimization_barrier((value, *earlier))[0]


def dot_tn(left, right):
    return lax.dot_general(left, right, (((0,), (0,)), ((), ())), preferred_element_type=F32)


def dot_nt(left, right):
    return lax.dot_general(left, right, (((1,), (1,)), ((), ())), preferred_element_type=F32)


def dot_nn(left, right):
    return jnp.dot(left, right, preferred_element_type=F32)


def call(kernel, outs, *operands, name, scalars=0, scratch=()):
    vmem, smem = pl.BlockSpec(memory_space=pltpu.VMEM), pl.BlockSpec(memory_space=pltpu.SMEM)
    specs = [smem] * scalars + [vmem] * (len(operands) - scalars)
    held = sum(math.prod(shape) * jnp.dtype(dtype).itemsize for shape, dtype in outs)
    held += sum(value.size * value.dtype.itemsize for value in operands)
    held += sum(math.prod(buffer.shape) * jnp.dtype(buffer.dtype).itemsize for buffer in scratch)
    return pl.pallas_call(
        kernel,
        out_shape=[jax.ShapeDtypeStruct(shape, dtype) for shape, dtype in outs],
        in_specs=specs,
        out_specs=[vmem] * len(outs),
        scratch_shapes=scratch,
        compiler_params=pltpu.CompilerParams(vmem_limit_bytes=min(held + 12 * 2**20, 56 * 2**20)),
        cost_estimate=pl.CostEstimate(flops=1, bytes_accessed=1, transcendentals=0),
        name=name,
    )(*operands)


def activate(places, preact, block):
    rows, inner = preact.shape
    count = inner // block

    def kernel(places_ref, preact_ref, *outs):
        for k in range(count):
            start = pl.multiple_of(places_ref[k] * block, 128)
            outs[k][...] = quick_gelu(preact_ref[:, pl.ds(start, block)].astype(F32)).astype(BF16)

    outs = [((rows, block), BF16)] * count
    return call(kernel, outs, places, preact, name="activate", scalars=1)


def score_rows(scale, mine, mate, others, device_count):
    rows, width, block = mine.shape[0], others.shape[0], 256

    def kernel(scale_ref, mine_ref, mate_ref, others_ref, lse, held):
        for half, ref in enumerate((mine_ref, mate_ref)):
            largest = None
            for place in range(0, width, block):
                part = scale_ref[0, 0] * dot_nt(ref[...], others_ref[place : place + block])
                held[half, :, place : place + block] = part
                here = jnp.max(part, axis=1, keepdims=True)
                largest = here if largest is None else jnp.maximum(largest, here)
            total = jnp.zeros_like(largest)
            for place in range(0, width, block):
                part = held[half, :, place : place + block]
                total += jnp.sum(jnp.exp(part - largest), axis=1, keepdims=True)
            value = jnp.broadcast_to(largest + jnp.log(total), (rows, 128))
            row = value.T[:1]
            for device in range(device_count):
                lse[device, :, half * rows : (half + 1) * rows] = row

    outs = [((device_count, 1, 2 * rows), F32)]
    scratch = [pltpu.VMEM((2, rows, width), F32)]
    return call(kernel, outs, scale, mine, mate, others, name="scores", scalars=1, scratch=scratch)[0]


def score_values(scale, mine, mate, others):
    rows, width, block = mine.shape[0], others.shape[0], 256

    def kernel(scale_ref, mine_ref, mate_ref, others_ref, *outs):
        for ref, out in zip((mine_ref, mate_ref), outs):
            for place in range(0, width, block):
                part = dot_nt(ref[...], others_ref[place : place + block])
                out[:, place : place + block] = scale_ref[0, 0] * part

    outs = [((rows, width), F32)] * 2
    return call(kernel, outs, scale, mine, mate, others, name="values", scalars=1)


def combine_lse(where, lse_all, count):
    rows = lse_all.shape[2] // 2

    def kernel(where_ref, lse_ref, column, row):
        def part(place, side):
            return lse_ref[where_ref[place]][:, side * rows : (side + 1) * rows]

        def log_add(left, right):
            top = jnp.maximum(left, right)
            return top + jnp.log(jnp.exp(left - top) + jnp.exp(right - top))

        for side in range(2):
            own = log_add(part(0, side), part(1, 1 - side))
            column[side * rows : (side + 1) * rows] = jnp.broadcast_to(own, (128, rows)).T[:, :1]
        for step in range(count):
            other = log_add(part(2 + 2 * step, 0), part(3 + 2 * step, 1))
            row[:, step * rows : (step + 1) * rows] = other

    outs = [((2 * rows, 1), F32), ((1, count * rows), F32)]
    return call(kernel, outs, where, lse_all, name="combine", scalars=1)


def all_terms(places, proj_own, rights, streams, embeds, columns):
    pieces, depth, width = len(embeds), proj_own.shape[0], rights[0][0].shape[1]
    rows, count = embeds[0].shape[0], len(rights) + 1

    def kernel(places_ref, proj_ref, *refs):
        embeds, refs = refs[:pieces], refs[pieces:]
        groups = [refs[pieces * i : pieces * (i + 1)] for i in range(len(rights))]
        streams, outs = refs[pieces * len(rights) :][: pieces // 2], refs[pieces * len(rights) + pieces // 2 :]
        left = outs[-1]
        for i, ref in enumerate(embeds):
            turned = dot_nt(proj_ref[...], ref[...]).astype(BF16)
            left[:, i * rows : (i + 1) * rows] = turned
        for i, group in enumerate(groups):
            total = None
            for j, ref in enumerate(group):
                part = dot_nn(left[:, j * rows : (j + 1) * rows], ref[...])
                total = part if total is None else total + part
            outs[i][:, :width] = total.astype(BF16)
        total = None
        for j, ref in enumerate(embeds):
            start = j % 2 * rows
            part = dot_nn(streams[j // 2][start : start + rows].T, ref[...])
            total = part if total is None else total + part
        for place in range(count):
            part = total[:, place * columns : (place + 1) * columns]
            for i in range(len(rights)):

                @pl.when(places_ref[i + 1] == place)
                def _():
                    outs[i][:, width:] = part.astype(BF16)

            @pl.when(places_ref[0] == place)
            def _():
                outs[-2][...] = part

    outs = [((depth, width + columns), BF16)] * len(rights)
    outs += [((depth, columns), F32), ((depth, rows * pieces), BF16)]
    flat = [piece for right in rights for piece in right]
    result = call(kernel, outs, places, proj_own, *embeds, *flat, *streams, name="terms", scalars=1)
    return result[:-2], result[-2], result[-1]


def weight_terms(left, right):
    depth, rows = left.shape[0], right[0].shape[0]

    def kernel(left_ref, *refs):
        out = refs[-1]
        total = None
        for j, ref in enumerate(refs[:-1]):
            part = dot_nn(left_ref[:, j * rows : (j + 1) * rows], ref[...])
            total = part if total is None else total + part
        out[...] = total

    return call(kernel, [((depth, right[0].shape[1]), F32)], left, *right, name="down_own")[0]


def own_gradients(places, found, preact, d_embed, proj_mine, proj_rest, down_mine, down_rest):
    rows, inner = preact.shape
    blocks = found.shape[0]
    count, block = len(down_mine), down_mine[0].shape[1]
    depth, half = proj_mine.shape[0], blocks // 2
    features = depth // half

    def kernel(places_ref, found_ref, preact_ref, embed_ref, proj_a, proj_b, *refs):
        down_a, down_b, (d_hidden, d_pre) = refs[:count], refs[count : 2 * count], refs[2 * count :]
        for i in range(blocks):
            place = found_ref[i]
            near = place < half
            start = pl.multiple_of(jnp.where(near, place, place - half) * features, 16)
            rows_a, rows_b = proj_a[pl.ds(start, features)], proj_b[pl.ds(start, features)]
            part = dot_nt(embed_ref[...], jnp.where(near, rows_a, rows_b)).astype(BF16)
            d_hidden[:, i * features : (i + 1) * features] = part
        left_a = dot_nt(embed_ref[...], proj_a[...]).astype(BF16)
        left_b = dot_nt(embed_ref[...], proj_b[...]).astype(BF16)
        for k in range(count):
            start = pl.multiple_of(places_ref[k] * block, 128)
            d_active = dot_nn(left_a, down_a[k][...]) + dot_nn(left_b, down_b[k][...])
            slope = gelu_slope(preact_ref[:, pl.ds(start, block)].astype(F32))
            d_pre[:, pl.ds(start, block)] = (d_active * slope).astype(BF16)

    return call(
        kernel, [((rows, blocks * features), BF16), (preact.shape, BF16)], places, found, preact, d_embed,
        proj_mine, proj_rest, *down_mine, *down_rest, name="own_gradients", scalars=2,
    )


def body(hidden, preact, w_down, projection, log_scale):
    tower_count = lax.axis_size("tower")
    grow_count, gcol_count = lax.axis_size("grow"), lax.axis_size("gcol")
    tower, grow, gcol = (lax.axis_index(a) for a in ("tower", "grow", "gcol"))
    hidden, preact, w_down, projection = hidden[0], preact[0], w_down[0], projection[0]
    features, inner_block = w_down.shape
    columns = projection.shape[1]
    js, ks = range(grow_count), range(gcol_count)
    evens = range(0, grow_count, 2)
    last = evens[-1]
    order = [(j, k) for j in evens for k in ks]
    sources = [lax.rem(gcol - k + gcol_count, gcol_count) for k in ks]
    far, core = (Lane(), Lane()), Lane()
    places = jnp.stack(sources)
    found = [((grow ^ j) >> 1) + ((grow ^ j) & 1) * (grow_count // 2) for j in js]
    places, found = lax.optimization_barrier((places, jnp.stack(found)))
    chunks = range(2)

    active = activate(places, preact, inner_block)
    down_ring = ring(w_down)
    proj_ring = [projection]
    for k in ks[1:]:
        pace = () if k == 1 else (down_ring[k - 1],)
        proj_ring.append(shift(after(proj_ring[-1], *pace), "gcol", 1))
    down_tables = [spread(part, far[0]) for part in down_ring]
    active_even = {1: spread(active[1])}
    proj_own = jnp.roll(jnp.concatenate(proj_ring[::-1], 1), (gcol + 1) * columns, 1)
    proj_even = spread(proj_own)
    proj_pair = jnp.concatenate([proj_even[j] for j in evens], 0)
    proj_mate = swap(proj_pair, "grow", 1)
    proj_all = jnp.concatenate([proj_pair, proj_mate], 0)
    down_pair = [jnp.concatenate([table[j] for j in evens], 0) for table in down_tables]
    active_mate = [core(part, 1) for part in active]
    hidden_parts = [
        lax.dynamic_slice_in_dim(hidden, (grow ^ j) * features, features, 1) for j in js
    ]
    hidden_mine = jnp.concatenate([hidden_parts[j] for j in evens], 1)
    hidden_mate = core(jnp.concatenate([hidden_parts[j + 1] for j in evens], 1), 1)

    stream = jnp.concatenate([hidden_mine, hidden_mate], 0).astype(F32)
    stream = stream + sum(
        dot_nt(jnp.concatenate([active[k], active_mate[k]], 0), down_pair[k]) for k in ks
    )
    stream = stream.astype(BF16)
    own_rows = hidden.shape[0]
    stream_rest = swap(stream[own_rows:], "grow", 1)
    stream_b = jnp.concatenate([stream[:own_rows], stream_rest], 1)
    embed = after(dot_nn(stream_b, proj_all), active_even[1][last])
    inverse = lax.rsqrt(jnp.sum(embed * embed, axis=1, keepdims=True) + 1e-06)
    unit = embed * inverse
    unit_b = unit.astype(BF16)

    (
        unit, unit_b, inverse, stream, proj_pair, proj_mate, proj_all, down_pair, active, active_mate, preact, active_even
    ) = lax.optimization_barrier(
        (unit, unit_b, inverse, stream, proj_pair, proj_mate, proj_all, down_pair, active, active_mate, preact, active_even)
    )
    far, core = (Lane(), Lane()), Lane()

    stream_blocks = [stream[:, i * features : (i + 1) * features] for i in range(len(evens))]
    stream_even = {0: stream_blocks[0]}
    for i, j in enumerate(evens[1:], 1):
        stream_even[j] = swap(stream_blocks[i], "grow", j)
    near = {j: swap_across(part) for j, part in spread(unit_b).items() if j}
    halves = jnp.split(unit_b, 2, 0)
    hops = [shift_across(part) for part in halves]
    across = near[0] = swap_across(after(unit_b, hops[0], stream_even[last]))
    rings = []
    for hop in hops:
        blocks = [None, hop]
        for k in ks[2:]:
            pace = (across,) if k == 3 else ()
            blocks.append(shift(after(blocks[-1], *pace), "gcol", 1))
        rings.append(blocks)
    unit_mate = swap(after(unit_b, rings[0][-1]), "grow", 1)
    pieces = [near] + [
        spread(jnp.concatenate([rings[q][k] for q in chunks], 0)) for k in ks[1:-1]
    ]
    lasts = [spread(after(rings[q][-1], pieces[1][last], near[last])) for q in chunks]
    pieces.append({j: jnp.concatenate([part[j] for part in lasts], 0) for j in evens})
    others = jnp.concatenate([pieces[k][j] for j, k in order], 0)
    device_count = tower_count * grow_count * gcol_count
    others, unit_mate, unit_b, active_even, stream_even, active, log_scale = lax.optimization_barrier(
        (others, unit_mate, unit_b, active_even, stream_even, active, log_scale)
    )
    logit_scale = jnp.exp(log_scale)
    lse = score_rows(logit_scale.reshape(1, 1), unit_b, unit_mate, others, device_count)
    scores_own, scores_mate = score_values(logit_scale.reshape(1, 1), unit_b, after(unit_mate, lse), others)
    lse_all = lax.all_to_all(lse, ("tower", "grow", "gcol"), 0, 0)

    far = (Lane(), Lane())
    for k in ks[2:]:
        active_even[k] = spread(active[k])
    core = Lane()
    active_odd = {k: {j: core(active_even[k][j], 1, others) for j in evens[1:]} for k in ks[1:]}

    def device(tower_of, j, k):
        return (tower_of * grow_count + (grow ^ j)) * gcol_count + sources[k]

    where = [device(tower, 0, 0), device(tower, 1, 0)]
    for j, k in order:
        where += [device(1 - tower, j, k), device(1 - tower, j ^ 1, k)]
    row_lse, other_lse = combine_lse(jnp.stack(where), lse_all, len(order))
    def embed_gradient(part, lse, diagonal):
        grad = 0.5 * (jnp.exp(part - lse) + jnp.exp(part - other_lse))
        return logit_scale * dot_nn((grad - diagonal).astype(BF16), others)

    row_index = lax.broadcasted_iota(jnp.int32, scores_own.shape, 0)
    column_index = lax.broadcasted_iota(jnp.int32, scores_own.shape, 1)
    diagonal = (row_index == column_index).astype(F32)
    arrived = [active_even[k][last] for k in ks[2:]]
    scores_mate, scores_own, row_lse = lax.optimization_barrier((scores_mate, scores_own, row_lse))
    for_mate = embed_gradient(after(scores_mate, *arrived), row_lse[own_rows:], 0.0)
    for_own = embed_gradient(after(scores_own, for_mate), row_lse[:own_rows], diagonal)
    d_unit = for_own + swap(for_mate, "grow", 1)
    along = jnp.sum(unit * d_unit, axis=1, keepdims=True)
    d_embed = (inverse * (d_unit - unit * along)).astype(BF16)
    for_barrier = (d_embed, active_even, active_odd, stream_even, down_pair, proj_all, for_mate)
    for_barrier = lax.optimization_barrier(for_barrier)
    d_embed, active_even, active_odd, stream_even, down_pair, proj_all, for_mate = for_barrier

    def right(k, even, odd):
        parts = {0: active[k], 1: active_mate[k]}
        for j in evens[1:]:
            parts[j], parts[j + 1] = even[j], odd[j]
        return [parts[j] for j in js]

    rights = {k: right(k, active_even[k], active_odd[k]) for k in ks[1:]}
    embed_rows = {}
    for j, part in spread(d_embed).items():
        embed_rows[j], embed_rows[j + 1] = part, swap(part, "grow", 1)
    down_mate = [swap(part, "grow", 1) for part in down_pair]
    away = [*ks[1:]]
    terms, grad_proj, left = all_terms(
        places, after(proj_pair[:features], *down_mate), [rights[k] for k in away], [stream_even[j] for j in evens],
        [embed_rows[j] for j in js], columns,
    )
    sent = [shift(term, "gcol", -k) for k, term in zip(away, terms)]
    even = spread(after(active[0], *terms))
    odd = {j: swap(even[j], "grow", 1) for j in evens[1:]}
    grad_down = weight_terms(left, right(0, even, odd))

    d_hidden, d_pre = own_gradients(
        places, found, preact, after(d_embed, *terms), proj_pair, proj_mate, down_pair, down_mate
    )
    grad_down, grad_proj = after(grad_down, d_pre, d_hidden), after(grad_proj, d_pre, d_hidden)
    for part in sent:
        grad_down = grad_down + part[:, :inner_block].astype(F32)
        grad_proj = grad_proj + part[:, inner_block:].astype(F32)
    return (d_hidden[None], d_pre[None], grad_down[None], grad_proj[None])


def solution(mesh):
    placed = (
        P("tower", ("grow", "gcol"), None),
        P("tower", ("grow", "gcol"), None),
        P("tower", "grow", "gcol"),
        P("tower", "grow", "gcol"),
        P(),
    )
    return jax.shard_map(
        body, mesh=mesh, in_specs=placed, out_specs=placed[:4], check_vma=False
    )
```

```python
import math

import jax
import jax.numpy as jnp
from jax import lax
from jax.experimental import pallas as pl
from jax.experimental.pallas import tpu as pltpu
from jax.sharding import PartitionSpec as P

F32 = jnp.float32
BF16 = jnp.bfloat16


def quick_gelu(values):
    return values * jax.nn.sigmoid(1.702 * values)


def gelu_slope(values):
    sigmoid = jax.nn.sigmoid(1.702 * values)
    return sigmoid + 1.702 * values * sigmoid * (1.0 - sigmoid)


def shift(value, axis, step):
    count = lax.axis_size(axis)
    return lax.ppermute(value, axis, [(i, (i + step) % count) for i in range(count)])


def swap(value, axis, bit):
    return lax.ppermute(value, axis, [(i, i ^ bit) for i in range(lax.axis_size(axis))])


def ring(value, *earlier):
    blocks = [value]
    for step in range(1, lax.axis_size("gcol")):
        part = after(blocks[-1], *earlier) if step == 2 and earlier else blocks[-1]
        blocks.append(shift(part, "gcol", 1))
    return blocks


def shift_across(value):
    towers, count = lax.axis_size("tower"), lax.axis_size("gcol")
    pairs = [
        (t * count + c, (towers - 1 - t) * count + (c + 1) % count)
        for t in range(towers)
        for c in range(count)
    ]
    return lax.ppermute(value, ("tower", "gcol"), pairs)


def swap_across(value):
    towers = lax.axis_size("tower")
    return lax.ppermute(value, "tower", [(t, towers - 1 - t) for t in range(towers)])


def grow_bits(last):
    bits, bit = [], lax.axis_size("grow") // 2
    while bit >= last:
        bits.append(bit)
        bit //= 2
    return bits


class Lane:
    def __init__(self):
        self.last = None

    def __call__(self, value, bit, *earlier):
        if self.last is not None:
            earlier = (*earlier, self.last)
        if earlier:
            value = after(value, *earlier)
        self.last = swap(value, "grow", bit)
        return self.last


def spread(value, lane=None, *earlier):
    table = {0: value}
    for bit in grow_bits(2):
        for j in list(table):
            table[j ^ bit] = lane(table[j], bit, *earlier) if lane else swap(table[j], "grow", bit)
    return table


def after(value, *earlier):
    return lax.optimization_barrier((value, *earlier))[0]


def dot_tn(left, right):
    return lax.dot_general(left, right, (((0,), (0,)), ((), ())), preferred_element_type=F32)


def dot_nt(left, right):
    return lax.dot_general(left, right, (((1,), (1,)), ((), ())), preferred_element_type=F32)


def dot_nn(left, right):
    return jnp.dot(left, right, preferred_element_type=F32)


def call(kernel, outs, *operands, name, scalars=0, scratch=()):
    vmem, smem = pl.BlockSpec(memory_space=pltpu.VMEM), pl.BlockSpec(memory_space=pltpu.SMEM)
    specs = [smem] * scalars + [vmem] * (len(operands) - scalars)
    held = sum(math.prod(shape) * jnp.dtype(dtype).itemsize for shape, dtype in outs)
    held += sum(value.size * value.dtype.itemsize for value in operands)
    held += sum(math.prod(buffer.shape) * jnp.dtype(buffer.dtype).itemsize for buffer in scratch)
    return pl.pallas_call(
        kernel,
        out_shape=[jax.ShapeDtypeStruct(shape, dtype) for shape, dtype in outs],
        in_specs=specs,
        out_specs=[vmem] * len(outs),
        scratch_shapes=scratch,
        compiler_params=pltpu.CompilerParams(vmem_limit_bytes=min(held + 12 * 2**20, 56 * 2**20)),
        cost_estimate=pl.CostEstimate(flops=1, bytes_accessed=1, transcendentals=0),
        name=name,
    )(*operands)


def activate(places, preact, block):
    rows, inner = preact.shape
    count = inner // block

    def kernel(places_ref, preact_ref, *outs):
        for k in range(count):
            start = pl.multiple_of(places_ref[k] * block, 128)
            outs[k][...] = quick_gelu(preact_ref[:, pl.ds(start, block)].astype(F32)).astype(BF16)

    outs = [((rows, block), BF16)] * count
    return call(kernel, outs, places, preact, name="activate", scalars=1)


def score_rows(scale, mine, mate, others, device_count):
    rows, width, block = mine.shape[0], others.shape[0], 256

    def kernel(scale_ref, mine_ref, mate_ref, others_ref, lse, held):
        for half, ref in enumerate((mine_ref, mate_ref)):
            largest = None
            for place in range(0, width, block):
                part = scale_ref[0, 0] * dot_nt(ref[...], others_ref[place : place + block])
                held[half, :, place : place + block] = part
                here = jnp.max(part, axis=1, keepdims=True)
                largest = here if largest is None else jnp.maximum(largest, here)
            total = jnp.zeros_like(largest)
            for place in range(0, width, block):
                part = held[half, :, place : place + block]
                total += jnp.sum(jnp.exp(part - largest), axis=1, keepdims=True)
            value = jnp.broadcast_to(largest + jnp.log(total), (rows, 128))
            row = value.T[:1]
            for device in range(device_count):
                lse[device, :, half * rows : (half + 1) * rows] = row

    outs = [((device_count, 1, 2 * rows), F32)]
    scratch = [pltpu.VMEM((2, rows, width), F32)]
    return call(kernel, outs, scale, mine, mate, others, name="scores", scalars=1, scratch=scratch)[0]


def score_values(scale, mine, mate, others):
    rows, width, block = mine.shape[0], others.shape[0], 256

    def kernel(scale_ref, mine_ref, mate_ref, others_ref, *outs):
        for ref, out in zip((mine_ref, mate_ref), outs):
            for place in range(0, width, block):
                part = dot_nt(ref[...], others_ref[place : place + block])
                out[:, place : place + block] = scale_ref[0, 0] * part

    outs = [((rows, width), F32)] * 2
    return call(kernel, outs, scale, mine, mate, others, name="values", scalars=1)


def combine_lse(where, lse_all, count):
    rows = lse_all.shape[2] // 2

    def kernel(where_ref, lse_ref, column, row):
        def part(place, side):
            return lse_ref[where_ref[place]][:, side * rows : (side + 1) * rows]

        def log_add(left, right):
            top = jnp.maximum(left, right)
            return top + jnp.log(jnp.exp(left - top) + jnp.exp(right - top))

        for side in range(2):
            own = log_add(part(0, side), part(1, 1 - side))
            column[side * rows : (side + 1) * rows] = jnp.broadcast_to(own, (128, rows)).T[:, :1]
        for step in range(count):
            other = log_add(part(2 + 2 * step, 0), part(3 + 2 * step, 1))
            row[:, step * rows : (step + 1) * rows] = other

    outs = [((2 * rows, 1), F32), ((1, count * rows), F32)]
    return call(kernel, outs, where, lse_all, name="combine", scalars=1)


def all_terms(places, proj_own, rights, streams, embeds, columns):
    pieces, depth, width = len(embeds), proj_own.shape[0], rights[0][0].shape[1]
    rows, count = embeds[0].shape[0], len(rights) + 1

    def kernel(places_ref, proj_ref, *refs):
        embeds, refs = refs[:pieces], refs[pieces:]
        groups = [refs[pieces * i : pieces * (i + 1)] for i in range(len(rights))]
        streams, outs = refs[pieces * len(rights) :][: pieces // 2], refs[pieces * len(rights) + pieces // 2 :]
        left = outs[-1]
        for i, ref in enumerate(embeds):
            turned = dot_nt(proj_ref[...], ref[...]).astype(BF16)
            left[:, i * rows : (i + 1) * rows] = turned
        for i, group in enumerate(groups):
            total = None
            for j, ref in enumerate(group):
                part = dot_nn(left[:, j * rows : (j + 1) * rows], ref[...])
                total = part if total is None else total + part
            outs[i][:, :width] = total.astype(BF16)
        total = None
        for j, ref in enumerate(embeds):
            start = j % 2 * rows
            part = dot_nn(streams[j // 2][start : start + rows].T, ref[...])
            total = part if total is None else total + part
        for place in range(count):
            part = total[:, place * columns : (place + 1) * columns]
            for i in range(len(rights)):

                @pl.when(places_ref[i + 1] == place)
                def _():
                    outs[i][:, width:] = part.astype(BF16)

            @pl.when(places_ref[0] == place)
            def _():
                outs[-2][...] = part

    outs = [((depth, width + columns), BF16)] * len(rights)
    outs += [((depth, columns), F32), ((depth, rows * pieces), BF16)]
    flat = [piece for right in rights for piece in right]
    result = call(kernel, outs, places, proj_own, *embeds, *flat, *streams, name="terms", scalars=1)
    return result[:-2], result[-2], result[-1]


def weight_terms(left, right):
    depth, rows = left.shape[0], right[0].shape[0]

    def kernel(left_ref, *refs):
        out = refs[-1]
        total = None
        for j, ref in enumerate(refs[:-1]):
            part = dot_nn(left_ref[:, j * rows : (j + 1) * rows], ref[...])
            total = part if total is None else total + part
        out[...] = total

    return call(kernel, [((depth, right[0].shape[1]), F32)], left, *right, name="down_own")[0]


def own_gradients(places, found, preact, d_embed, proj_mine, proj_rest, down_mine, down_rest):
    rows, inner = preact.shape
    blocks = found.shape[0]
    count, block = len(down_mine), down_mine[0].shape[1]
    depth, half = proj_mine.shape[0], blocks // 2
    features = depth // half

    def kernel(places_ref, found_ref, preact_ref, embed_ref, proj_a, proj_b, *refs):
        down_a, down_b, (d_hidden, d_pre) = refs[:count], refs[count : 2 * count], refs[2 * count :]
        for i in range(blocks):
            place = found_ref[i]
            near = place < half
            start = pl.multiple_of(jnp.where(near, place, place - half) * features, 16)
            rows_a, rows_b = proj_a[pl.ds(start, features)], proj_b[pl.ds(start, features)]
            part = dot_nt(embed_ref[...], jnp.where(near, rows_a, rows_b)).astype(BF16)
            d_hidden[:, i * features : (i + 1) * features] = part
        left_a = dot_nt(embed_ref[...], proj_a[...]).astype(BF16)
        left_b = dot_nt(embed_ref[...], proj_b[...]).astype(BF16)
        for k in range(count):
            start = pl.multiple_of(places_ref[k] * block, 128)
            d_active = dot_nn(left_a, down_a[k][...]) + dot_nn(left_b, down_b[k][...])
            slope = gelu_slope(preact_ref[:, pl.ds(start, block)].astype(F32))
            d_pre[:, pl.ds(start, block)] = (d_active * slope).astype(BF16)

    return call(
        kernel, [((rows, blocks * features), BF16), (preact.shape, BF16)], places, found, preact, d_embed,
        proj_mine, proj_rest, *down_mine, *down_rest, name="own_gradients", scalars=2,
    )


def body(hidden, preact, w_down, projection, log_scale):
    tower_count = lax.axis_size("tower")
    grow_count, gcol_count = lax.axis_size("grow"), lax.axis_size("gcol")
    tower, grow, gcol = (lax.axis_index(a) for a in ("tower", "grow", "gcol"))
    hidden, preact, w_down, projection = hidden[0], preact[0], w_down[0], projection[0]
    features, inner_block = w_down.shape
    columns = projection.shape[1]
    js, ks = range(grow_count), range(gcol_count)
    evens = range(0, grow_count, 2)
    last = evens[-1]
    order = [(j, k) for j in evens for k in ks]
    sources = [lax.rem(gcol - k + gcol_count, gcol_count) for k in ks]
    far, core = (Lane(), Lane()), Lane()
    places = jnp.stack(sources)
    found = [((grow ^ j) >> 1) + ((grow ^ j) & 1) * (grow_count // 2) for j in js]
    places, found = lax.optimization_barrier((places, jnp.stack(found)))
    chunks = range(2)

    active = activate(places, preact, inner_block)
    down_ring = ring(w_down)
    proj_ring = [projection]
    for k in ks[1:]:
        pace = () if k == 1 else (down_ring[k - 1],)
        proj_ring.append(shift(after(proj_ring[-1], *pace), "gcol", 1))
    down_tables = [spread(part, far[0]) for part in down_ring]
    active_even = {1: spread(after(active[1], down_tables[0][last]))}
    proj_own = jnp.roll(jnp.concatenate(proj_ring[::-1], 1), (gcol + 1) * columns, 1)
    proj_even = spread(proj_own)
    proj_pair = jnp.concatenate([proj_even[j] for j in evens], 0)
    proj_mate = swap(proj_pair, "grow", 1)
    proj_all = jnp.concatenate([proj_pair, proj_mate], 0)
    down_pair = [jnp.concatenate([table[j] for j in evens], 0) for table in down_tables]
    active_mate = [core(part, 1) for part in active]
    hidden_parts = [
        lax.dynamic_slice_in_dim(hidden, (grow ^ j) * features, features, 1) for j in js
    ]
    hidden_mine = jnp.concatenate([hidden_parts[j] for j in evens], 1)
    hidden_mate = core(jnp.concatenate([hidden_parts[j + 1] for j in evens], 1), 1)

    stream = jnp.concatenate([hidden_mine, hidden_mate], 0).astype(F32)
    stream = stream + sum(
        dot_nt(jnp.concatenate([active[k], active_mate[k]], 0), down_pair[k]) for k in ks
    )
    stream = stream.astype(BF16)
    own_rows = hidden.shape[0]
    stream_rest = swap(stream[own_rows:], "grow", 1)
    stream_b = jnp.concatenate([stream[:own_rows], stream_rest], 1)
    embed = after(dot_nn(stream_b, proj_all), active_even[1][last])
    inverse = lax.rsqrt(jnp.sum(embed * embed, axis=1, keepdims=True) + 1e-06)
    unit = embed * inverse
    unit_b = unit.astype(BF16)

    stream_blocks = [stream[:, i * features : (i + 1) * features] for i in range(len(evens))]
    (
        unit, unit_b, inverse, stream_blocks, proj_pair, proj_mate, proj_all, down_pair, active, active_mate, preact, active_even
    ) = lax.optimization_barrier(
        (unit, unit_b, inverse, stream_blocks, proj_pair, proj_mate, proj_all, down_pair, active, active_mate, preact, active_even)
    )
    far, core = (Lane(), Lane()), Lane()

    stream_even = {0: stream_blocks[0]}
    for i, j in enumerate(evens[1:], 1):
        stream_even[j] = swap(stream_blocks[i], "grow", j)
    near = {j: swap_across(part) for j, part in spread(unit_b).items() if j}
    halves = jnp.split(unit_b, 2, 0)
    hops = [shift_across(part) for part in halves]
    across = near[0] = swap_across(after(unit_b, hops[0], stream_even[last]))
    rings = []
    for hop in hops:
        blocks = [None, hop]
        for k in ks[2:]:
            pace = (across,) if k == 3 else ()
            blocks.append(shift(after(blocks[-1], *pace), "gcol", 1))
        rings.append(blocks)
    unit_mate = swap(after(unit_b, rings[0][-1]), "grow", 1)
    pieces = [near] + [
        spread(jnp.concatenate([rings[q][k] for q in chunks], 0)) for k in ks[1:-1]
    ]
    lasts = [spread(after(rings[q][-1], pieces[1][last], near[last])) for q in chunks]
    pieces.append({j: jnp.concatenate([part[j] for part in lasts], 0) for j in evens})
    others = jnp.concatenate([pieces[k][j] for j, k in order], 0)
    device_count = tower_count * grow_count * gcol_count
    others, unit_mate, unit_b, active_even, stream_even, active, log_scale = lax.optimization_barrier(
        (others, unit_mate, unit_b, active_even, stream_even, active, log_scale)
    )
    logit_scale = jnp.exp(log_scale)
    lse = score_rows(logit_scale.reshape(1, 1), unit_b, unit_mate, others, device_count)
    scores_own, scores_mate = score_values(logit_scale.reshape(1, 1), unit_b, after(unit_mate, lse), others)
    lse_all = lax.all_to_all(lse, ("tower", "grow", "gcol"), 0, 0)

    far = (Lane(), Lane())
    for k in ks[2:]:
        active_even[k] = spread(active[k])
    core = Lane()
    active_odd = {k: {j: core(active_even[k][j], 1, others) for j in evens[1:]} for k in ks[1:]}

    def device(tower_of, j, k):
        return (tower_of * grow_count + (grow ^ j)) * gcol_count + sources[k]

    where = [device(tower, 0, 0), device(tower, 1, 0)]
    for j, k in order:
        where += [device(1 - tower, j, k), device(1 - tower, j ^ 1, k)]
    row_lse, other_lse = combine_lse(jnp.stack(where), lse_all, len(order))
    def embed_gradient(part, lse, diagonal):
        grad = 0.5 * (jnp.exp(part - lse) + jnp.exp(part - other_lse))
        return logit_scale * dot_nn((grad - diagonal).astype(BF16), others)

    row_index = lax.broadcasted_iota(jnp.int32, scores_own.shape, 0)
    column_index = lax.broadcasted_iota(jnp.int32, scores_own.shape, 1)
    diagonal = (row_index == column_index).astype(F32)
    arrived = [active_even[k][last] for k in ks[2:]]
    scores_mate, scores_own, row_lse = lax.optimization_barrier((scores_mate, scores_own, row_lse))
    for_mate = embed_gradient(after(scores_mate, *arrived), row_lse[own_rows:], 0.0)
    for_own = embed_gradient(after(scores_own, for_mate), row_lse[:own_rows], diagonal)
    d_unit = for_own + swap(for_mate, "grow", 1)
    along = jnp.sum(unit * d_unit, axis=1, keepdims=True)
    d_embed = (inverse * (d_unit - unit * along)).astype(BF16)
    for_barrier = (d_embed, active_even, active_odd, stream_even, down_pair, proj_all, for_mate)
    for_barrier = lax.optimization_barrier(for_barrier)
    d_embed, active_even, active_odd, stream_even, down_pair, proj_all, for_mate = for_barrier

    def right(k, even, odd):
        parts = {0: active[k], 1: active_mate[k]}
        for j in evens[1:]:
            parts[j], parts[j + 1] = even[j], odd[j]
        return [parts[j] for j in js]

    rights = {k: right(k, active_even[k], active_odd[k]) for k in ks[1:]}
    embed_rows = {}
    for j, part in spread(d_embed).items():
        embed_rows[j], embed_rows[j + 1] = part, swap(part, "grow", 1)
    down_mate = [swap(part, "grow", 1) for part in down_pair]
    away = [*ks[1:]]
    terms, grad_proj, left = all_terms(
        places, after(proj_pair[:features], *down_mate), [rights[k] for k in away], [stream_even[j] for j in evens],
        [embed_rows[j] for j in js], columns,
    )
    sent = [shift(term, "gcol", -k) for k, term in zip(away, terms)]
    even = spread(after(active[0], *terms))
    odd = {j: swap(even[j], "grow", 1) for j in evens[1:]}
    grad_down = weight_terms(left, right(0, even, odd))

    d_hidden, d_pre = own_gradients(
        places, found, preact, after(d_embed, *terms), proj_pair, proj_mate, down_pair, down_mate
    )
    grad_down, grad_proj = after(grad_down, d_pre, d_hidden), after(grad_proj, d_pre, d_hidden)
    for part in sent:
        grad_down = grad_down + part[:, :inner_block].astype(F32)
        grad_proj = grad_proj + part[:, inner_block:].astype(F32)
    return (d_hidden[None], d_pre[None], grad_down[None], grad_proj[None])


def solution(mesh):
    placed = (
        P("tower", ("grow", "gcol"), None),
        P("tower", ("grow", "gcol"), None),
        P("tower", "grow", "gcol"),
        P("tower", "grow", "gcol"),
        P(),
    )
    return jax.shard_map(
        body, mesh=mesh, in_specs=placed, out_specs=placed[:4], check_vma=False
    )
```

```python
import math

import jax
import jax.numpy as jnp
from jax import lax
from jax.experimental import pallas as pl
from jax.experimental.pallas import tpu as pltpu
from jax.sharding import PartitionSpec as P

F32 = jnp.float32
BF16 = jnp.bfloat16


def quick_gelu(values):
    return values * jax.nn.sigmoid(1.702 * values)


def gelu_slope(values):
    sigmoid = jax.nn.sigmoid(1.702 * values)
    return sigmoid + 1.702 * values * sigmoid * (1.0 - sigmoid)


def shift(value, axis, step):
    count = lax.axis_size(axis)
    return lax.ppermute(value, axis, [(i, (i + step) % count) for i in range(count)])


def swap(value, axis, bit):
    return lax.ppermute(value, axis, [(i, i ^ bit) for i in range(lax.axis_size(axis))])


def ring(value, *earlier):
    blocks = [value]
    for step in range(1, lax.axis_size("gcol")):
        part = after(blocks[-1], *earlier) if step == 2 and earlier else blocks[-1]
        blocks.append(shift(part, "gcol", 1))
    return blocks


def shift_across(value):
    towers, count = lax.axis_size("tower"), lax.axis_size("gcol")
    pairs = [
        (t * count + c, (towers - 1 - t) * count + (c + 1) % count)
        for t in range(towers)
        for c in range(count)
    ]
    return lax.ppermute(value, ("tower", "gcol"), pairs)


def swap_across(value):
    towers = lax.axis_size("tower")
    return lax.ppermute(value, "tower", [(t, towers - 1 - t) for t in range(towers)])


def grow_bits(last):
    bits, bit = [], lax.axis_size("grow") // 2
    while bit >= last:
        bits.append(bit)
        bit //= 2
    return bits


class Lane:
    def __init__(self):
        self.last = None

    def __call__(self, value, bit, *earlier):
        if self.last is not None:
            earlier = (*earlier, self.last)
        if earlier:
            value = after(value, *earlier)
        self.last = swap(value, "grow", bit)
        return self.last


def spread(value, lane=None, *earlier):
    table = {0: value}
    for bit in grow_bits(2):
        for j in list(table):
            table[j ^ bit] = lane(table[j], bit, *earlier) if lane else swap(table[j], "grow", bit)
    return table


def after(value, *earlier):
    return lax.optimization_barrier((value, *earlier))[0]


def dot_tn(left, right):
    return lax.dot_general(left, right, (((0,), (0,)), ((), ())), preferred_element_type=F32)


def dot_nt(left, right):
    return lax.dot_general(left, right, (((1,), (1,)), ((), ())), preferred_element_type=F32)


def dot_nn(left, right):
    return jnp.dot(left, right, preferred_element_type=F32)


def call(kernel, outs, *operands, name, scalars=0, scratch=()):
    vmem, smem = pl.BlockSpec(memory_space=pltpu.VMEM), pl.BlockSpec(memory_space=pltpu.SMEM)
    specs = [smem] * scalars + [vmem] * (len(operands) - scalars)
    held = sum(math.prod(shape) * jnp.dtype(dtype).itemsize for shape, dtype in outs)
    held += sum(value.size * value.dtype.itemsize for value in operands)
    held += sum(math.prod(buffer.shape) * jnp.dtype(buffer.dtype).itemsize for buffer in scratch)
    return pl.pallas_call(
        kernel,
        out_shape=[jax.ShapeDtypeStruct(shape, dtype) for shape, dtype in outs],
        in_specs=specs,
        out_specs=[vmem] * len(outs),
        scratch_shapes=scratch,
        compiler_params=pltpu.CompilerParams(vmem_limit_bytes=min(held + 12 * 2**20, 56 * 2**20)),
        cost_estimate=pl.CostEstimate(flops=1, bytes_accessed=1, transcendentals=0),
        name=name,
    )(*operands)


def activate(places, preact, block):
    rows, inner = preact.shape
    count = inner // block

    def kernel(places_ref, preact_ref, *outs):
        for k in range(count):
            start = pl.multiple_of(places_ref[k] * block, 128)
            outs[k][...] = quick_gelu(preact_ref[:, pl.ds(start, block)].astype(F32)).astype(BF16)

    outs = [((rows, block), BF16)] * count
    return call(kernel, outs, places, preact, name="activate", scalars=1)


def score_rows(scale, mine, mate, others, device_count):
    rows, width, block = mine.shape[0], others.shape[0], 256

    def kernel(scale_ref, mine_ref, mate_ref, others_ref, lse, held):
        for half, ref in enumerate((mine_ref, mate_ref)):
            largest = None
            for place in range(0, width, block):
                part = scale_ref[0, 0] * dot_nt(ref[...], others_ref[place : place + block])
                held[half, :, place : place + block] = part
                here = jnp.max(part, axis=1, keepdims=True)
                largest = here if largest is None else jnp.maximum(largest, here)
            total = jnp.zeros_like(largest)
            for place in range(0, width, block):
                part = held[half, :, place : place + block]
                total += jnp.sum(jnp.exp(part - largest), axis=1, keepdims=True)
            value = jnp.broadcast_to(largest + jnp.log(total), (rows, 128))
            row = value.T[:1]
            for device in range(device_count):
                lse[device, :, half * rows : (half + 1) * rows] = row

    outs = [((device_count, 1, 2 * rows), F32)]
    scratch = [pltpu.VMEM((2, rows, width), F32)]
    return call(kernel, outs, scale, mine, mate, others, name="scores", scalars=1, scratch=scratch)[0]


def score_values(scale, mine, mate, others):
    rows, width, block = mine.shape[0], others.shape[0], 256

    def kernel(scale_ref, mine_ref, mate_ref, others_ref, *outs):
        for ref, out in zip((mine_ref, mate_ref), outs):
            for place in range(0, width, block):
                part = dot_nt(ref[...], others_ref[place : place + block])
                out[:, place : place + block] = scale_ref[0, 0] * part

    outs = [((rows, width), F32)] * 2
    return call(kernel, outs, scale, mine, mate, others, name="values", scalars=1)


def combine_lse(where, lse_all, count):
    rows = lse_all.shape[2] // 2

    def kernel(where_ref, lse_ref, column, row):
        def part(place, side):
            return lse_ref[where_ref[place]][:, side * rows : (side + 1) * rows]

        def log_add(left, right):
            top = jnp.maximum(left, right)
            return top + jnp.log(jnp.exp(left - top) + jnp.exp(right - top))

        for side in range(2):
            own = log_add(part(0, side), part(1, 1 - side))
            column[side * rows : (side + 1) * rows] = jnp.broadcast_to(own, (128, rows)).T[:, :1]
        for step in range(count):
            other = log_add(part(2 + 2 * step, 0), part(3 + 2 * step, 1))
            row[:, step * rows : (step + 1) * rows] = other

    outs = [((2 * rows, 1), F32), ((1, count * rows), F32)]
    return call(kernel, outs, where, lse_all, name="combine", scalars=1)


def all_terms(places, proj_own, rights, streams, embeds, columns):
    pieces, depth, width = len(embeds), proj_own.shape[0], rights[0][0].shape[1]
    rows, count = embeds[0].shape[0], len(rights) + 1

    def kernel(places_ref, proj_ref, *refs):
        embeds, refs = refs[:pieces], refs[pieces:]
        groups = [refs[pieces * i : pieces * (i + 1)] for i in range(len(rights))]
        streams, outs = refs[pieces * len(rights) :][: pieces // 2], refs[pieces * len(rights) + pieces // 2 :]
        left = outs[-1]
        for i, ref in enumerate(embeds):
            turned = dot_nt(proj_ref[...], ref[...]).astype(BF16)
            left[:, i * rows : (i + 1) * rows] = turned
        for i, group in enumerate(groups):
            total = None
            for j, ref in enumerate(group):
                part = dot_nn(left[:, j * rows : (j + 1) * rows], ref[...])
                total = part if total is None else total + part
            outs[i][:, :width] = total.astype(BF16)
        total = None
        for j, ref in enumerate(embeds):
            start = j % 2 * rows
            part = dot_nn(streams[j // 2][start : start + rows].T, ref[...])
            total = part if total is None else total + part
        for place in range(count):
            part = total[:, place * columns : (place + 1) * columns]
            for i in range(len(rights)):

                @pl.when(places_ref[i + 1] == place)
                def _():
                    outs[i][:, width:] = part.astype(BF16)

            @pl.when(places_ref[0] == place)
            def _():
                outs[-2][...] = part

    outs = [((depth, width + columns), BF16)] * len(rights)
    outs += [((depth, columns), F32), ((depth, rows * pieces), BF16)]
    flat = [piece for right in rights for piece in right]
    result = call(kernel, outs, places, proj_own, *embeds, *flat, *streams, name="terms", scalars=1)
    return result[:-2], result[-2], result[-1]


def weight_terms(left, right):
    depth, rows = left.shape[0], right[0].shape[0]

    def kernel(left_ref, *refs):
        out = refs[-1]
        total = None
        for j, ref in enumerate(refs[:-1]):
            part = dot_nn(left_ref[:, j * rows : (j + 1) * rows], ref[...])
            total = part if total is None else total + part
        out[...] = total

    return call(kernel, [((depth, right[0].shape[1]), F32)], left, *right, name="down_own")[0]


def own_gradients(places, found, preact, d_embed, proj_mine, proj_rest, down_mine, down_rest):
    rows, inner = preact.shape
    blocks = found.shape[0]
    count, block = len(down_mine), down_mine[0].shape[1]
    depth, half = proj_mine.shape[0], blocks // 2
    features = depth // half

    def kernel(places_ref, found_ref, preact_ref, embed_ref, proj_a, proj_b, *refs):
        down_a, down_b, (d_hidden, d_pre) = refs[:count], refs[count : 2 * count], refs[2 * count :]
        for i in range(blocks):
            place = found_ref[i]
            near = place < half
            start = pl.multiple_of(jnp.where(near, place, place - half) * features, 16)
            rows_a, rows_b = proj_a[pl.ds(start, features)], proj_b[pl.ds(start, features)]
            part = dot_nt(embed_ref[...], jnp.where(near, rows_a, rows_b)).astype(BF16)
            d_hidden[:, i * features : (i + 1) * features] = part
        left_a = dot_nt(embed_ref[...], proj_a[...]).astype(BF16)
        left_b = dot_nt(embed_ref[...], proj_b[...]).astype(BF16)
        for k in range(count):
            start = pl.multiple_of(places_ref[k] * block, 128)
            d_active = dot_nn(left_a, down_a[k][...]) + dot_nn(left_b, down_b[k][...])
            slope = gelu_slope(preact_ref[:, pl.ds(start, block)].astype(F32))
            d_pre[:, pl.ds(start, block)] = (d_active * slope).astype(BF16)

    return call(
        kernel, [((rows, blocks * features), BF16), (preact.shape, BF16)], places, found, preact, d_embed,
        proj_mine, proj_rest, *down_mine, *down_rest, name="own_gradients", scalars=2,
    )


def body(hidden, preact, w_down, projection, log_scale):
    tower_count = lax.axis_size("tower")
    grow_count, gcol_count = lax.axis_size("grow"), lax.axis_size("gcol")
    tower, grow, gcol = (lax.axis_index(a) for a in ("tower", "grow", "gcol"))
    hidden, preact, w_down, projection = hidden[0], preact[0], w_down[0], projection[0]
    features, inner_block = w_down.shape
    columns = projection.shape[1]
    js, ks = range(grow_count), range(gcol_count)
    evens = range(0, grow_count, 2)
    last = evens[-1]
    order = [(j, k) for j in evens for k in ks]
    sources = [lax.rem(gcol - k + gcol_count, gcol_count) for k in ks]
    far, core = (Lane(), Lane()), Lane()
    places = jnp.stack(sources)
    found = [((grow ^ j) >> 1) + ((grow ^ j) & 1) * (grow_count // 2) for j in js]
    places, found = lax.optimization_barrier((places, jnp.stack(found)))
    chunks = range(2)

    active = activate(places, preact, inner_block)
    down_ring = ring(w_down)
    proj_ring = [projection]
    for k in ks[1:]:
        pace = () if k == 1 else (down_ring[k - 1],)
        proj_ring.append(shift(after(proj_ring[-1], *pace), "gcol", 1))
    down_tables = [spread(part, far[0]) for part in down_ring]
    active_even = {1: spread(after(active[1], down_tables[0][last]))}
    proj_own = jnp.roll(jnp.concatenate(proj_ring[::-1], 1), (gcol + 1) * columns, 1)
    proj_even = spread(proj_own)
    proj_pair = jnp.concatenate([proj_even[j] for j in evens], 0)
    proj_mate = swap(proj_pair, "grow", 1)
    proj_all = jnp.concatenate([proj_pair, proj_mate], 0)
    down_pair = [jnp.concatenate([table[j] for j in evens], 0) for table in down_tables]
    active_mate = [core(part, 1) for part in active]
    hidden_parts = [
        lax.dynamic_slice_in_dim(hidden, (grow ^ j) * features, features, 1) for j in js
    ]
    hidden_mine = jnp.concatenate([hidden_parts[j] for j in evens], 1)
    hidden_mate = core(jnp.concatenate([hidden_parts[j + 1] for j in evens], 1), 1)

    stream = jnp.concatenate([hidden_mine, hidden_mate], 0).astype(F32)
    stream = stream + sum(
        dot_nt(jnp.concatenate([active[k], active_mate[k]], 0), down_pair[k]) for k in ks
    )
    stream = stream.astype(BF16)
    own_rows = hidden.shape[0]
    stream_rest = swap(stream[own_rows:], "grow", 1)
    stream_b = jnp.concatenate([stream[:own_rows], stream_rest], 1)
    embed = after(dot_nn(stream_b, proj_all), active_even[1][last])
    inverse = lax.rsqrt(jnp.sum(embed * embed, axis=1, keepdims=True) + 1e-06)
    unit = embed * inverse
    unit_b = unit.astype(BF16)

    stream_blocks = [stream[:, i * features : (i + 1) * features] for i in range(len(evens))]
    (
        unit, unit_b, inverse, stream_blocks, proj_pair, proj_mate, proj_all, down_pair, active, active_mate, preact, active_even
    ) = lax.optimization_barrier(
        (unit, unit_b, inverse, stream_blocks, proj_pair, proj_mate, proj_all, down_pair, active, active_mate, preact, active_even)
    )
    far, core = (Lane(), Lane()), Lane()

    stream_even = {0: stream_blocks[0]}
    for i, j in enumerate(evens[1:], 1):
        stream_even[j] = swap(stream_blocks[i], "grow", j)
    near = {j: swap_across(part) for j, part in spread(unit_b).items() if j}
    halves = jnp.split(unit_b, 2, 0)
    hops = [shift_across(part) for part in halves]
    across = near[0] = swap_across(after(unit_b, hops[0], stream_even[last]))
    rings = []
    for hop in hops:
        blocks = [None, hop]
        for k in ks[2:]:
            pace = ()
            blocks.append(shift(after(blocks[-1], *pace), "gcol", 1))
        rings.append(blocks)
    unit_mate = swap(after(unit_b, rings[0][-1]), "grow", 1)
    pieces = [near] + [
        spread(jnp.concatenate([rings[q][k] for q in chunks], 0)) for k in ks[1:-1]
    ]
    lasts = [spread(after(rings[q][-1], pieces[1][last], near[last])) for q in chunks]
    pieces.append({j: jnp.concatenate([part[j] for part in lasts], 0) for j in evens})
    others = jnp.concatenate([pieces[k][j] for j, k in order], 0)
    device_count = tower_count * grow_count * gcol_count
    others, unit_mate, unit_b, active_even, stream_even, active, log_scale = lax.optimization_barrier(
        (others, unit_mate, unit_b, active_even, stream_even, active, log_scale)
    )
    logit_scale = jnp.exp(log_scale)
    lse = score_rows(logit_scale.reshape(1, 1), unit_b, unit_mate, others, device_count)
    scores_own, scores_mate = score_values(logit_scale.reshape(1, 1), unit_b, after(unit_mate, lse), others)
    lse_all = lax.all_to_all(lse, ("tower", "grow", "gcol"), 0, 0)

    far = (Lane(), Lane())
    for k in ks[2:]:
        active_even[k] = spread(active[k])
    core = Lane()
    active_odd = {k: {j: core(active_even[k][j], 1, others) for j in evens[1:]} for k in ks[1:]}

    def device(tower_of, j, k):
        return (tower_of * grow_count + (grow ^ j)) * gcol_count + sources[k]

    where = [device(tower, 0, 0), device(tower, 1, 0)]
    for j, k in order:
        where += [device(1 - tower, j, k), device(1 - tower, j ^ 1, k)]
    row_lse, other_lse = combine_lse(jnp.stack(where), lse_all, len(order))
    def embed_gradient(part, lse, diagonal):
        grad = 0.5 * (jnp.exp(part - lse) + jnp.exp(part - other_lse))
        return logit_scale * dot_nn((grad - diagonal).astype(BF16), others)

    row_index = lax.broadcasted_iota(jnp.int32, scores_own.shape, 0)
    column_index = lax.broadcasted_iota(jnp.int32, scores_own.shape, 1)
    diagonal = (row_index == column_index).astype(F32)
    arrived = [active_even[k][last] for k in ks[2:]]
    scores_mate, scores_own, row_lse = lax.optimization_barrier((scores_mate, scores_own, row_lse))
    for_mate = embed_gradient(after(scores_mate, *arrived), row_lse[own_rows:], 0.0)
    for_own = embed_gradient(after(scores_own, for_mate), row_lse[:own_rows], diagonal)
    d_unit = for_own + swap(for_mate, "grow", 1)
    along = jnp.sum(unit * d_unit, axis=1, keepdims=True)
    d_embed = (inverse * (d_unit - unit * along)).astype(BF16)
    for_barrier = (d_embed, active_even, active_odd, stream_even, down_pair, proj_all, for_mate)
    for_barrier = lax.optimization_barrier(for_barrier)
    d_embed, active_even, active_odd, stream_even, down_pair, proj_all, for_mate = for_barrier

    def right(k, even, odd):
        parts = {0: active[k], 1: active_mate[k]}
        for j in evens[1:]:
            parts[j], parts[j + 1] = even[j], odd[j]
        return [parts[j] for j in js]

    rights = {k: right(k, active_even[k], active_odd[k]) for k in ks[1:]}
    embed_rows = {}
    for j, part in spread(d_embed).items():
        embed_rows[j], embed_rows[j + 1] = part, swap(part, "grow", 1)
    down_mate = [swap(part, "grow", 1) for part in down_pair]
    away = [*ks[1:]]
    terms, grad_proj, left = all_terms(
        places, after(proj_pair[:features], *down_mate), [rights[k] for k in away], [stream_even[j] for j in evens],
        [embed_rows[j] for j in js], columns,
    )
    sent = [shift(term, "gcol", -k) for k, term in zip(away, terms)]
    even = spread(after(active[0], *terms))
    odd = {j: swap(even[j], "grow", 1) for j in evens[1:]}
    grad_down = weight_terms(left, right(0, even, odd))

    d_hidden, d_pre = own_gradients(
        places, found, preact, after(d_embed, *terms), proj_pair, proj_mate, down_pair, down_mate
    )
    grad_down, grad_proj = after(grad_down, d_pre, d_hidden), after(grad_proj, d_pre, d_hidden)
    for part in sent:
        grad_down = grad_down + part[:, :inner_block].astype(F32)
        grad_proj = grad_proj + part[:, inner_block:].astype(F32)
    return (d_hidden[None], d_pre[None], grad_down[None], grad_proj[None])


def solution(mesh):
    placed = (
        P("tower", ("grow", "gcol"), None),
        P("tower", ("grow", "gcol"), None),
        P("tower", "grow", "gcol"),
        P("tower", "grow", "gcol"),
        P(),
    )
    return jax.shard_map(
        body, mesh=mesh, in_specs=placed, out_specs=placed[:4], check_vma=False
    )
```

```python
import math

import jax
import jax.numpy as jnp
from jax import lax
from jax.experimental import pallas as pl
from jax.experimental.pallas import tpu as pltpu
from jax.sharding import PartitionSpec as P

F32 = jnp.float32
BF16 = jnp.bfloat16


def quick_gelu(values):
    return values * jax.nn.sigmoid(1.702 * values)


def gelu_slope(values):
    sigmoid = jax.nn.sigmoid(1.702 * values)
    return sigmoid + 1.702 * values * sigmoid * (1.0 - sigmoid)


def shift(value, axis, step):
    count = lax.axis_size(axis)
    return lax.ppermute(value, axis, [(i, (i + step) % count) for i in range(count)])


def swap(value, axis, bit):
    return lax.ppermute(value, axis, [(i, i ^ bit) for i in range(lax.axis_size(axis))])


def ring(value, *earlier):
    blocks = [value]
    for step in range(1, lax.axis_size("gcol")):
        part = after(blocks[-1], *earlier) if step == 2 and earlier else blocks[-1]
        blocks.append(shift(part, "gcol", 1))
    return blocks


def shift_across(value):
    towers, count = lax.axis_size("tower"), lax.axis_size("gcol")
    pairs = [
        (t * count + c, (towers - 1 - t) * count + (c + 1) % count)
        for t in range(towers)
        for c in range(count)
    ]
    return lax.ppermute(value, ("tower", "gcol"), pairs)


def swap_across(value):
    towers = lax.axis_size("tower")
    return lax.ppermute(value, "tower", [(t, towers - 1 - t) for t in range(towers)])


def grow_bits(last):
    bits, bit = [], lax.axis_size("grow") // 2
    while bit >= last:
        bits.append(bit)
        bit //= 2
    return bits


class Lane:
    def __init__(self):
        self.last = None

    def __call__(self, value, bit, *earlier):
        if self.last is not None:
            earlier = (*earlier, self.last)
        if earlier:
            value = after(value, *earlier)
        self.last = swap(value, "grow", bit)
        return self.last


def spread(value, lane=None, *earlier):
    table = {0: value}
    for bit in grow_bits(2):
        for j in list(table):
            table[j ^ bit] = lane(table[j], bit, *earlier) if lane else swap(table[j], "grow", bit)
    return table


def after(value, *earlier):
    return lax.optimization_barrier((value, *earlier))[0]


def dot_tn(left, right):
    return lax.dot_general(left, right, (((0,), (0,)), ((), ())), preferred_element_type=F32)


def dot_nt(left, right):
    return lax.dot_general(left, right, (((1,), (1,)), ((), ())), preferred_element_type=F32)


def dot_nn(left, right):
    return jnp.dot(left, right, preferred_element_type=F32)


def call(kernel, outs, *operands, name, scalars=0, scratch=()):
    vmem, smem = pl.BlockSpec(memory_space=pltpu.VMEM), pl.BlockSpec(memory_space=pltpu.SMEM)
    specs = [smem] * scalars + [vmem] * (len(operands) - scalars)
    held = sum(math.prod(shape) * jnp.dtype(dtype).itemsize for shape, dtype in outs)
    held += sum(value.size * value.dtype.itemsize for value in operands)
    held += sum(math.prod(buffer.shape) * jnp.dtype(buffer.dtype).itemsize for buffer in scratch)
    return pl.pallas_call(
        kernel,
        out_shape=[jax.ShapeDtypeStruct(shape, dtype) for shape, dtype in outs],
        in_specs=specs,
        out_specs=[vmem] * len(outs),
        scratch_shapes=scratch,
        compiler_params=pltpu.CompilerParams(vmem_limit_bytes=min(held + 12 * 2**20, 56 * 2**20)),
        cost_estimate=pl.CostEstimate(flops=1, bytes_accessed=1, transcendentals=0),
        name=name,
    )(*operands)


def activate(places, preact, block):
    rows, inner = preact.shape
    count = inner // block

    def kernel(places_ref, preact_ref, *outs):
        for k in range(count):
            start = pl.multiple_of(places_ref[k] * block, 128)
            outs[k][...] = quick_gelu(preact_ref[:, pl.ds(start, block)].astype(F32)).astype(BF16)

    outs = [((rows, block), BF16)] * count
    return call(kernel, outs, places, preact, name="activate", scalars=1)


def score_rows(scale, mine, mate, others, device_count):
    rows, width, block = mine.shape[0], others.shape[0], 256

    def kernel(scale_ref, mine_ref, mate_ref, others_ref, lse, held):
        for half, ref in enumerate((mine_ref, mate_ref)):
            largest = None
            for place in range(0, width, block):
                part = scale_ref[0, 0] * dot_nt(ref[...], others_ref[place : place + block])
                held[half, :, place : place + block] = part
                here = jnp.max(part, axis=1, keepdims=True)
                largest = here if largest is None else jnp.maximum(largest, here)
            total = jnp.zeros_like(largest)
            for place in range(0, width, block):
                part = held[half, :, place : place + block]
                total += jnp.sum(jnp.exp(part - largest), axis=1, keepdims=True)
            value = jnp.broadcast_to(largest + jnp.log(total), (rows, 128))
            row = value.T[:1]
            for device in range(device_count):
                lse[device, :, half * rows : (half + 1) * rows] = row

    outs = [((device_count, 1, 2 * rows), F32)]
    scratch = [pltpu.VMEM((2, rows, width), F32)]
    return call(kernel, outs, scale, mine, mate, others, name="scores", scalars=1, scratch=scratch)[0]


def score_values(scale, mine, mate, others):
    rows, width, block = mine.shape[0], others.shape[0], 256

    def kernel(scale_ref, mine_ref, mate_ref, others_ref, *outs):
        for ref, out in zip((mine_ref, mate_ref), outs):
            for place in range(0, width, block):
                part = dot_nt(ref[...], others_ref[place : place + block])
                out[:, place : place + block] = scale_ref[0, 0] * part

    outs = [((rows, width), F32)] * 2
    return call(kernel, outs, scale, mine, mate, others, name="values", scalars=1)


def combine_lse(where, lse_all, count):
    rows = lse_all.shape[2] // 2

    def kernel(where_ref, lse_ref, column, row):
        def part(place, side):
            return lse_ref[where_ref[place]][:, side * rows : (side + 1) * rows]

        def log_add(left, right):
            top = jnp.maximum(left, right)
            return top + jnp.log(jnp.exp(left - top) + jnp.exp(right - top))

        for side in range(2):
            own = log_add(part(0, side), part(1, 1 - side))
            column[side * rows : (side + 1) * rows] = jnp.broadcast_to(own, (128, rows)).T[:, :1]
        for step in range(count):
            other = log_add(part(2 + 2 * step, 0), part(3 + 2 * step, 1))
            row[:, step * rows : (step + 1) * rows] = other

    outs = [((2 * rows, 1), F32), ((1, count * rows), F32)]
    return call(kernel, outs, where, lse_all, name="combine", scalars=1)


def all_terms(places, proj_own, rights, streams, embeds, columns):
    pieces, depth, width = len(embeds), proj_own.shape[0], rights[0][0].shape[1]
    rows, count = embeds[0].shape[0], len(rights) + 1

    def kernel(places_ref, proj_ref, *refs):
        embeds, refs = refs[:pieces], refs[pieces:]
        groups = [refs[pieces * i : pieces * (i + 1)] for i in range(len(rights))]
        streams, outs = refs[pieces * len(rights) :][: pieces // 2], refs[pieces * len(rights) + pieces // 2 :]
        left = outs[-1]
        for i, ref in enumerate(embeds):
            turned = dot_nt(proj_ref[...], ref[...]).astype(BF16)
            left[:, i * rows : (i + 1) * rows] = turned
        for i, group in enumerate(groups):
            total = None
            for j, ref in enumerate(group):
                part = dot_nn(left[:, j * rows : (j + 1) * rows], ref[...])
                total = part if total is None else total + part
            outs[i][:, :width] = total.astype(BF16)
        total = None
        for j, ref in enumerate(embeds):
            start = j % 2 * rows
            part = dot_nn(streams[j // 2][start : start + rows].T, ref[...])
            total = part if total is None else total + part
        for place in range(count):
            part = total[:, place * columns : (place + 1) * columns]
            for i in range(len(rights)):

                @pl.when(places_ref[i + 1] == place)
                def _():
                    outs[i][:, width:] = part.astype(BF16)

            @pl.when(places_ref[0] == place)
            def _():
                outs[-2][...] = part

    outs = [((depth, width + columns), BF16)] * len(rights)
    outs += [((depth, columns), F32), ((depth, rows * pieces), BF16)]
    flat = [piece for right in rights for piece in right]
    result = call(kernel, outs, places, proj_own, *embeds, *flat, *streams, name="terms", scalars=1)
    return result[:-2], result[-2], result[-1]


def weight_terms(left, right):
    depth, rows = left.shape[0], right[0].shape[0]

    def kernel(left_ref, *refs):
        out = refs[-1]
        total = None
        for j, ref in enumerate(refs[:-1]):
            part = dot_nn(left_ref[:, j * rows : (j + 1) * rows], ref[...])
            total = part if total is None else total + part
        out[...] = total

    return call(kernel, [((depth, right[0].shape[1]), F32)], left, *right, name="down_own")[0]


def own_gradients(places, found, preact, d_embed, proj_mine, proj_rest, down_mine, down_rest):
    rows, inner = preact.shape
    blocks = found.shape[0]
    count, block = len(down_mine), down_mine[0].shape[1]
    depth, half = proj_mine.shape[0], blocks // 2
    features = depth // half

    def kernel(places_ref, found_ref, preact_ref, embed_ref, proj_a, proj_b, *refs):
        down_a, down_b, (d_hidden, d_pre) = refs[:count], refs[count : 2 * count], refs[2 * count :]
        for i in range(blocks):
            place = found_ref[i]
            near = place < half
            start = pl.multiple_of(jnp.where(near, place, place - half) * features, 16)
            rows_a, rows_b = proj_a[pl.ds(start, features)], proj_b[pl.ds(start, features)]
            part = dot_nt(embed_ref[...], jnp.where(near, rows_a, rows_b)).astype(BF16)
            d_hidden[:, i * features : (i + 1) * features] = part
        left_a = dot_nt(embed_ref[...], proj_a[...]).astype(BF16)
        left_b = dot_nt(embed_ref[...], proj_b[...]).astype(BF16)
        for k in range(count):
            start = pl.multiple_of(places_ref[k] * block, 128)
            d_active = dot_nn(left_a, down_a[k][...]) + dot_nn(left_b, down_b[k][...])
            slope = gelu_slope(preact_ref[:, pl.ds(start, block)].astype(F32))
            d_pre[:, pl.ds(start, block)] = (d_active * slope).astype(BF16)

    return call(
        kernel, [((rows, blocks * features), BF16), (preact.shape, BF16)], places, found, preact, d_embed,
        proj_mine, proj_rest, *down_mine, *down_rest, name="own_gradients", scalars=2,
    )


def body(hidden, preact, w_down, projection, log_scale):
    tower_count = lax.axis_size("tower")
    grow_count, gcol_count = lax.axis_size("grow"), lax.axis_size("gcol")
    tower, grow, gcol = (lax.axis_index(a) for a in ("tower", "grow", "gcol"))
    hidden, preact, w_down, projection = hidden[0], preact[0], w_down[0], projection[0]
    features, inner_block = w_down.shape
    columns = projection.shape[1]
    js, ks = range(grow_count), range(gcol_count)
    evens = range(0, grow_count, 2)
    last = evens[-1]
    order = [(j, k) for j in evens for k in ks]
    sources = [lax.rem(gcol - k + gcol_count, gcol_count) for k in ks]
    far, core = (Lane(), Lane()), Lane()
    places = jnp.stack(sources)
    found = [((grow ^ j) >> 1) + ((grow ^ j) & 1) * (grow_count // 2) for j in js]
    places, found = lax.optimization_barrier((places, jnp.stack(found)))
    chunks = range(2)

    active = activate(places, preact, inner_block)
    down_ring = ring(w_down)
    proj_ring = [projection]
    for k in ks[1:]:
        pace = () if k == 1 else (down_ring[k - 1],)
        proj_ring.append(shift(after(proj_ring[-1], *pace), "gcol", 1))
    down_tables = [spread(part, far[0]) for part in down_ring]
    active_even = {1: spread(after(active[1], down_ring[1]))}
    proj_own = jnp.roll(jnp.concatenate(proj_ring[::-1], 1), (gcol + 1) * columns, 1)
    proj_even = spread(proj_own)
    proj_pair = jnp.concatenate([proj_even[j] for j in evens], 0)
    proj_mate = swap(proj_pair, "grow", 1)
    proj_all = jnp.concatenate([proj_pair, proj_mate], 0)
    down_pair = [jnp.concatenate([table[j] for j in evens], 0) for table in down_tables]
    active_mate = [core(part, 1) for part in active]
    hidden_parts = [
        lax.dynamic_slice_in_dim(hidden, (grow ^ j) * features, features, 1) for j in js
    ]
    hidden_mine = jnp.concatenate([hidden_parts[j] for j in evens], 1)
    hidden_mate = core(jnp.concatenate([hidden_parts[j + 1] for j in evens], 1), 1)

    stream = jnp.concatenate([hidden_mine, hidden_mate], 0).astype(F32)
    stream = stream + sum(
        dot_nt(jnp.concatenate([active[k], active_mate[k]], 0), down_pair[k]) for k in ks
    )
    stream = stream.astype(BF16)
    own_rows = hidden.shape[0]
    stream_rest = swap(stream[own_rows:], "grow", 1)
    stream_b = jnp.concatenate([stream[:own_rows], stream_rest], 1)
    embed = after(dot_nn(stream_b, proj_all), active_even[1][last])
    inverse = lax.rsqrt(jnp.sum(embed * embed, axis=1, keepdims=True) + 1e-06)
    unit = embed * inverse
    unit_b = unit.astype(BF16)

    stream_blocks = [stream[:, i * features : (i + 1) * features] for i in range(len(evens))]
    (
        unit, unit_b, inverse, stream_blocks, proj_pair, proj_mate, proj_all, down_pair, active, active_mate, preact, active_even
    ) = lax.optimization_barrier(
        (unit, unit_b, inverse, stream_blocks, proj_pair, proj_mate, proj_all, down_pair, active, active_mate, preact, active_even)
    )
    far, core = (Lane(), Lane()), Lane()

    stream_even = {0: stream_blocks[0]}
    for i, j in enumerate(evens[1:], 1):
        stream_even[j] = swap(stream_blocks[i], "grow", j)
    near = {j: swap_across(part) for j, part in spread(unit_b).items() if j}
    halves = jnp.split(unit_b, 2, 0)
    hops = [shift_across(part) for part in halves]
    across = near[0] = swap_across(after(unit_b, hops[0], stream_even[last]))
    rings = []
    for hop in hops:
        blocks = [None, hop]
        for k in ks[2:]:
            pace = (across,) if k == 3 else ()
            blocks.append(shift(after(blocks[-1], *pace), "gcol", 1))
        rings.append(blocks)
    unit_mate = swap(after(unit_b, rings[0][-1]), "grow", 1)
    pieces = [near] + [
        spread(jnp.concatenate([rings[q][k] for q in chunks], 0)) for k in ks[1:-1]
    ]
    lasts = [spread(after(rings[q][-1], pieces[1][last], near[last])) for q in chunks]
    pieces.append({j: jnp.concatenate([part[j] for part in lasts], 0) for j in evens})
    others = jnp.concatenate([pieces[k][j] for j, k in order], 0)
    device_count = tower_count * grow_count * gcol_count
    others, unit_mate, unit_b, active_even, stream_even, active, log_scale = lax.optimization_barrier(
        (others, unit_mate, unit_b, active_even, stream_even, active, log_scale)
    )
    logit_scale = jnp.exp(log_scale)
    lse = score_rows(logit_scale.reshape(1, 1), unit_b, unit_mate, others, device_count)
    scores_own, scores_mate = score_values(logit_scale.reshape(1, 1), unit_b, after(unit_mate, lse), others)
    lse_all = lax.all_to_all(lse, ("tower", "grow", "gcol"), 0, 0)

    far = (Lane(), Lane())
    for k in ks[2:]:
        active_even[k] = spread(active[k])
    core = Lane()
    active_odd = {k: {j: core(active_even[k][j], 1, others) for j in evens[1:]} for k in ks[1:]}

    def device(tower_of, j, k):
        return (tower_of * grow_count + (grow ^ j)) * gcol_count + sources[k]

    where = [device(tower, 0, 0), device(tower, 1, 0)]
    for j, k in order:
        where += [device(1 - tower, j, k), device(1 - tower, j ^ 1, k)]
    row_lse, other_lse = combine_lse(jnp.stack(where), lse_all, len(order))
    def embed_gradient(part, lse, diagonal):
        grad = 0.5 * (jnp.exp(part - lse) + jnp.exp(part - other_lse))
        return logit_scale * dot_nn((grad - diagonal).astype(BF16), others)

    row_index = lax.broadcasted_iota(jnp.int32, scores_own.shape, 0)
    column_index = lax.broadcasted_iota(jnp.int32, scores_own.shape, 1)
    diagonal = (row_index == column_index).astype(F32)
    arrived = [active_even[k][last] for k in ks[2:]]
    scores_mate, scores_own, row_lse = lax.optimization_barrier((scores_mate, scores_own, row_lse))
    for_mate = embed_gradient(after(scores_mate, *arrived), row_lse[own_rows:], 0.0)
    for_own = embed_gradient(after(scores_own, for_mate), row_lse[:own_rows], diagonal)
    d_unit = for_own + swap(for_mate, "grow", 1)
    along = jnp.sum(unit * d_unit, axis=1, keepdims=True)
    d_embed = (inverse * (d_unit - unit * along)).astype(BF16)
    for_barrier = (d_embed, active_even, active_odd, stream_even, down_pair, proj_all, for_mate)
    for_barrier = lax.optimization_barrier(for_barrier)
    d_embed, active_even, active_odd, stream_even, down_pair, proj_all, for_mate = for_barrier

    def right(k, even, odd):
        parts = {0: active[k], 1: active_mate[k]}
        for j in evens[1:]:
            parts[j], parts[j + 1] = even[j], odd[j]
        return [parts[j] for j in js]

    rights = {k: right(k, active_even[k], active_odd[k]) for k in ks[1:]}
    embed_rows = {}
    for j, part in spread(d_embed).items():
        embed_rows[j], embed_rows[j + 1] = part, swap(part, "grow", 1)
    down_mate = [swap(part, "grow", 1) for part in down_pair]
    away = [*ks[1:]]
    terms, grad_proj, left = all_terms(
        places, after(proj_pair[:features], *down_mate), [rights[k] for k in away], [stream_even[j] for j in evens],
        [embed_rows[j] for j in js], columns,
    )
    sent = [shift(term, "gcol", -k) for k, term in zip(away, terms)]
    even = spread(after(active[0], *terms))
    odd = {j: swap(even[j], "grow", 1) for j in evens[1:]}
    grad_down = weight_terms(left, right(0, even, odd))

    d_hidden, d_pre = own_gradients(
        places, found, preact, after(d_embed, *terms), proj_pair, proj_mate, down_pair, down_mate
    )
    grad_down, grad_proj = after(grad_down, d_pre, d_hidden), after(grad_proj, d_pre, d_hidden)
    for part in sent:
        grad_down = grad_down + part[:, :inner_block].astype(F32)
        grad_proj = grad_proj + part[:, inner_block:].astype(F32)
    return (d_hidden[None], d_pre[None], grad_down[None], grad_proj[None])


def solution(mesh):
    placed = (
        P("tower", ("grow", "gcol"), None),
        P("tower", ("grow", "gcol"), None),
        P("tower", "grow", "gcol"),
        P("tower", "grow", "gcol"),
        P(),
    )
    return jax.shard_map(
        body, mesh=mesh, in_specs=placed, out_specs=placed[:4], check_vma=False
    )
```
